512 devices in a mesh: gz: 8 (over y, core), row: 8 (over x, z_hi), col: 8 (over z_lo).
Axes of the slice: x: 4, y: 4, z: 16 (z_hi: 2, z_lo: 8; z = z_hi * 8 + z_lo), core: 2. Of those that a mesh axis runs over, the one named last changes fastest.
Arguments:
- contributions: bfloat16 [8, 8192, 8192], P('gz', 'row', 'col'), may hold values from -1.5 to 1.5
- block_pattern: int32 [32, 32], replicated, may hold values 0 or 1
- row_map: int32 [32], replicated, may hold values from 0 to 31, each once
- col_map: int32 [32], replicated, may hold values from 0 to 31, each once
- lower_inv: float32 [2, 256, 256], replicated, may hold values from -1 to 1, as said below
- upper_inv: float32 [2, 256, 256], replicated, may hold values from -2 to 2, as said below
Outputs:
- factored: bfloat16 [8192, 8192], P('row', ('col', 'gz'))
The draws below stay inside these ranges and needn't reach their ends.
Inputs may be any that keep to these rules, and one draw needn't show every extreme that they name: `row_map`: each block index appears once. `col_map`: each block index appears once. `lower_inv`: zero above the diagonal, ones on it. `upper_inv`: zero below the diagonal, diagonal entries from 0.5 to 2.
All inputs are finite; a program needn't handle non-finite values.
Results may differ from the reference program's by a relative error of at most 0.0012.
Values sent between devices are 32-bit elements; how exact they have to be, the bound alone decides.
No kernel may reach another device: no remote copies, remote signals or barrier semaphores. Data moves between devices by JAX's collectives and lax.ppermute only.
A program may use at most 64 MiB of HBM per device.

```python
import jax
import jax.numpy as jnp
from jax import lax

B = 256
NBLK = 32
N_GZ = 8


def draw_lower_inv(key, part):
    key = jax.random.fold_in(key, 7)
    values = jnp.clip(jax.random.normal(key, (2, B, B), jnp.float32), -4.0, 4.0) * 0.5 / jnp.sqrt(1.0 * B)
    strict = jnp.tril(jnp.ones((B, B), jnp.float32), -1)
    return values * strict[None] + jnp.eye(B, dtype=jnp.float32)[None]


def draw_upper_inv(key, part):
    key = jax.random.fold_in(key, 11)
    first, second = jax.random.split(key)
    values = jnp.clip(jax.random.normal(first, (2, B, B), jnp.float32), -4.0, 4.0) * 0.5 / jnp.sqrt(1.0 * B)
    diagonal = jnp.exp(jax.random.uniform(second, (2, B), jnp.float32, jnp.log(0.5), jnp.log(2.0)))
    strict = jnp.triu(jnp.ones((B, B), jnp.float32), 1)
    return values * strict[None] + diagonal[:, :, None] * jnp.eye(B, dtype=jnp.float32)[None]


def plant(result, key, least, high):
    longest = result.shape.index(max(result.shape))
    spots = []
    for shift in (0, 1):
        where = [jax.random.randint(jax.random.fold_in(key, axis), (), 0, length) for axis, length in enumerate(result.shape)]
        where[longest] = (where[longest] + shift) % result.shape[longest]
        spots.append(tuple(where))
    return result.at[spots[0]].set(least).at[spots[1]].set(high)


def levels(stream_key, dims, cuts, least, largest):
    def one(dim, shards_of):
        draws = jax.random.uniform(jax.random.fold_in(jax.random.fold_in(stream_key, 6), dim), (shards_of,), jnp.float32, least / len(cuts), largest / len(cuts))
        return jnp.repeat(jnp.exp(draws), dims[dim] // shards_of).reshape((-1,) + (1,) * (len(dims) - dim - 1))

    loudness = one(*cuts[0])
    for cut in cuts[1:]:
        loudness = loudness * one(*cut)
    return loudness


def gaussian(own_key, dims, spread, limit, cuts=(), kind=jnp.bfloat16):
    level = levels(own_key, dims, cuts, -0.22, 0.18) if cuts else 1.0
    array = jax.random.normal(own_key, dims, jnp.float32) * spread * level
    return jnp.minimum(jnp.maximum(array, -limit), limit).astype(kind)


def setup_inputs(seed: int = 0) -> dict:
    streams_of = jax.random.split(jax.random.key(seed), 7)
    return {
        "contributions": gaussian(streams_of[0], (N_GZ, NBLK * B, NBLK * B), 0.1, 1.5, ((0, 8), (1, 8), (2, 8))),
        "block_pattern": plant((jax.random.randint(streams_of[1], (NBLK, NBLK), 0, 5) < 3).astype(jnp.int32), jax.random.fold_in(streams_of[1], 1), 0, 1),
        "row_map": jax.random.permutation(streams_of[2], NBLK).astype(jnp.int32),
        "col_map": jax.random.permutation(streams_of[3], NBLK).astype(jnp.int32),
        "lower_inv": draw_lower_inv(jax.random.fold_in(streams_of[6], 71), 0),
        "upper_inv": draw_upper_inv(jax.random.fold_in(streams_of[6], 71), 0),
    }


def position_of(table, value):
    iota = jnp.arange(table.shape[0], dtype=jnp.int32)
    return jnp.sum(jnp.where(table == value, iota, 0)).astype(jnp.int32)


def reference(contributions, block_pattern, row_map, col_map, lower_inv, upper_inv):
    highest = lax.Precision.HIGHEST
    block_count = row_map.shape[0]
    block_size = upper_inv.shape[-1]
    summed = contributions[0].astype(jnp.float32)
    for layer in range(1, contributions.shape[0]):
        summed = summed + contributions[layer].astype(jnp.float32)
    pattern_f = jnp.maximum(block_pattern, jnp.eye(block_count, dtype=jnp.int32)).astype(jnp.float32)
    pattern_st = pattern_f[row_map][:, col_map]
    matrix = summed.reshape(block_count, block_size, block_count, block_size) * pattern_st[:, None, :, None]
    for pivot_step in range(2):
        pivot_row = position_of(row_map, pivot_step)
        pivot_col = position_of(col_map, pivot_step)
        row_keep = (row_map > pivot_step)
        col_keep = (col_map > pivot_step)
        column_blocks = jnp.take(matrix, pivot_col, axis=2)
        low_panel = jnp.einsum("pab,bc->pac", column_blocks, upper_inv[pivot_step], precision=highest)
        low_panel = low_panel * row_keep.astype(jnp.float32)[:, None, None]
        row_blocks = jnp.take(matrix, pivot_row, axis=0)
        up_panel = jnp.einsum("ab,bqc->aqc", lower_inv[pivot_step], row_blocks, precision=highest)
        up_panel = up_panel * col_keep.astype(jnp.float32)[None, :, None]
        update = jnp.dot(low_panel.reshape(block_count * block_size, block_size),
                         up_panel.reshape(block_size, block_count * block_size), precision=highest)
        update = update.reshape(block_count, block_size, block_count, block_size)
        matrix = matrix - pattern_st[:, None, :, None] * update
        new_column = jnp.where(row_keep[:, None, None], low_panel, jnp.take(matrix, pivot_col, axis=2))
        matrix = matrix.at[:, :, pivot_col, :].set(new_column)
        new_row = jnp.where(col_keep[None, :, None], up_panel, jnp.take(matrix, pivot_row, axis=0))
        matrix = matrix.at[pivot_row].set(new_row)
    return matrix.reshape(block_count * block_size, block_count * block_size).astype(jnp.bfloat16)
```

```python
import jax
import jax.numpy as jnp
from jax import lax
from jax.sharding import PartitionSpec as P

HIGHEST = lax.Precision.HIGHEST


def lookup(index, table):
    iota = jnp.arange(table.shape[0], dtype=jnp.int32)
    return jnp.sum(jnp.where(index == iota, table, 0))


def position_of(table, value):
    iota = jnp.arange(table.shape[0], dtype=jnp.int32)
    return jnp.sum(jnp.where(table == value, iota, 0)).astype(jnp.int32)


def mm(a, b):
    return jnp.dot(a, b, precision=HIGHEST)


def swap(x, axis, size, bit):
    return lax.ppermute(x, axis, [(i, i ^ bit) for i in range(size)])


def bit_of(index, bit):
    return (index // bit) % 2


def part(x, axis, which):
    half = x.shape[axis] // 2
    return lax.dynamic_slice_in_dim(x, which * half, half, axis)


def join(mine, other, axis, which):
    return jnp.where(
        which == 0,
        jnp.concatenate([mine, other], axis),
        jnp.concatenate([other, mine], axis),
    )


def choose(mine, other, me, sources, bit):
    same = [bit_of(me, bit) == bit_of(s, bit) for s in sources]
    return jnp.stack([jnp.where(same[k], mine[k], other[k]) for k in range(2)])


def spread(data, axis, size, me, sources, near, far, cross):
    for bit in (near, far):
        which = bit_of(me, bit)
        other = swap(part(data, 1, 1 - which), axis, size, bit)
        data = choose(part(data, 1, which), other, me, sources, bit)
    other = swap(data, axis, size, cross)
    data = choose(data, other, me, sources, cross)
    for bit in (far, near):
        which = bit_of(me, bit)
        data = join(data, swap(data, axis, size, bit), 1, which)
    return data


def shards(contributions, block_pattern, row_map, col_map, lower_inv, upper_inv):
    size = upper_inv.shape[-1]
    local = contributions[0]
    slots = local.shape[0] // size
    count = block_pattern.shape[0]
    n_gz, n_row, n_col = lax.axis_size("gz"), lax.axis_size("row"), lax.axis_size("col")
    gz, row, col = lax.axis_index("gz"), lax.axis_index("row"), lax.axis_index("col")
    y, core = gz // 2, gz % 2
    n_y = n_gz // 2
    thin = size // n_gz
    row_at = [position_of(row_map, k) for k in range(2)]
    col_at = [position_of(col_map, k) for k in range(2)]
    row_owner = [p // slots for p in row_at]
    col_owner = [p // slots for p in col_at]
    pattern = jnp.maximum(block_pattern, jnp.eye(count, dtype=jnp.int32)).astype(jnp.float32)

    merged = lax.psum_scatter(local.astype(jnp.float32), "gz", scatter_dimension=1, tiled=True)
    width = merged.shape[1]

    panel = jnp.stack(
        [
            lax.dynamic_slice_in_dim(local, (p % slots) * size, size, 1).astype(jnp.float32)
            for p in col_at
        ]
    )
    panel = panel.reshape(2, slots, n_y, 2, thin, size)
    keep = lax.dynamic_index_in_dim(panel, core, 3, keepdims=False)
    give = lax.dynamic_index_in_dim(panel, 1 - core, 3, keepdims=False)
    panel = keep + swap(give, "gz", n_gz, 1)
    total = lax.dynamic_index_in_dim(panel, y, 2, keepdims=False)
    for step in (1, 3, 2):
        chunk = lax.dynamic_index_in_dim(panel, (y + step) % n_y, 2, keepdims=False)
        total = total + lax.ppermute(
            chunk, "gz", [(2 * i + c, 2 * ((i + step) % n_y) + c) for i in range(n_y) for c in range(2)]
        )

    corner = jnp.stack(
        [
            lax.dynamic_index_in_dim(total[k], row_at[1 - k] % slots, 0, keepdims=False)
            for k in range(2)
        ]
    )
    for bit in (1, 2, 4):
        corner = choose(corner, swap(corner, "row", n_row, bit), row, row_owner[::-1], bit)
    for bit in (4, 2, 1):
        corner = choose(corner, swap(corner, "col", n_col, bit), col, col_owner, bit)

    panel = spread(total.reshape(2, slots * thin, size), "col", n_col, col, col_owner, 1, 2, 4)
    mine = jnp.concatenate([panel, corner], 1)
    both = lax.all_gather(mine, "gz", axis=0)
    both = both.reshape(n_gz, 2, slots + 1, thin, size).transpose(1, 2, 0, 3, 4)
    both = both.reshape(2, slots + 1, size, size)
    raw = both[:, :slots].reshape(2, slots * size, size)
    below, above = both[0, slots], both[1, slots]

    blocks = merged.reshape(slots, size, width)
    rows = jnp.stack(
        [lax.dynamic_index_in_dim(blocks, p % slots, 0, keepdims=False) for p in row_at]
    )
    rows = spread(rows, "row", n_row, row, row_owner, 2, 4, 1)

    col_first = col * local.shape[1] + gz * width
    offset = col_first % size
    col_global = lookup(col_first // size, col_map)
    row_global = jnp.stack([lookup(row * slots + s, row_map) for s in range(slots)])
    pattern_col = jnp.sum(
        jnp.where(jnp.arange(count) == col_global, pattern, 0.0), axis=1
    )
    hot = (row_global[:, None] == jnp.arange(count)).astype(jnp.float32)
    pattern_own = jnp.sum(hot * pattern_col, axis=1)
    keep = [
        (row_global > k).astype(jnp.float32) * jnp.sum(hot * pattern[:, k], axis=1)
        for k in range(2)
    ]
    keep = [jnp.repeat(k, size)[:, None] for k in keep]

    low0 = keep[0] * mm(raw[0], upper_inv[0])
    low0_at = pattern[1, 0] * mm(below, upper_inv[0])
    up0_at = pattern[0, 1] * mm(lower_inv[0], above)
    low1 = keep[1] * mm(raw[1] - mm(low0, up0_at), upper_inv[1])
    up0 = jnp.where(col_global > 0, pattern_col[0], 0.0) * mm(lower_inv[0], rows[0])
    up1 = jnp.where(col_global > 1, pattern_col[1], 0.0) * mm(
        lower_inv[1], rows[1] - mm(low0_at, up0)
    )
    update = (mm(low0, up0) + mm(low1, up1)).reshape(slots, size, width)
    matrix = pattern_own[:, None, None] * (blocks - update)
    lows = [
        lax.dynamic_slice_in_dim(low, offset, width, 1).reshape(slots, size, width)
        for low in (low0, low1)
    ]
    rg = row_global[:, None, None]
    matrix = jnp.where((col_global == 0) & (rg > 0), lows[0], matrix)
    matrix = jnp.where((col_global == 1) & (rg > 1), lows[1], matrix)
    matrix = jnp.where((rg == 0) & (col_global > 0), up0[None], matrix)
    matrix = jnp.where((rg == 1) & (col_global > 1), up1[None], matrix)
    return matrix.reshape(slots * size, width).astype(jnp.bfloat16)


def solution(mesh):
    in_specs = (P("gz", "row", "col"), P(), P(), P(), P(), P())
    out_specs = P("row", ("col", "gz"))
    return jax.shard_map(shards, mesh=mesh, in_specs=in_specs, out_specs=out_specs, check_vma=False)
```

```python
import functools

import jax
import jax.numpy as jnp
from jax import lax
from jax.experimental import pallas as pl
from jax.experimental.pallas import tpu as pltpu
from jax.sharding import PartitionSpec as P

VMEM = pl.BlockSpec(memory_space=pltpu.VMEM)
SMEM = pl.BlockSpec(memory_space=pltpu.SMEM)
PARAMS = pltpu.CompilerParams(vmem_limit_bytes=32 << 20)


def position_of(table, value):
    iota = jnp.arange(table.shape[0], dtype=jnp.uint32)
    return jnp.sum(jnp.where(table == value, iota, 0), dtype=jnp.uint32)


def halves(a):
    high = a.astype(jnp.bfloat16)
    return high, (a - high.astype(jnp.float32)).astype(jnp.bfloat16)


def mm_halves(a, b):
    dot = functools.partial(jnp.dot, preferred_element_type=jnp.float32)
    return dot(a[0], b[0]) + (dot(a[0], b[1]) + dot(a[1], b[0]))


def mm(a, b):
    return mm_halves(halves(a), halves(b))


def find(ref, value):
    place = jnp.int32(0)
    for i in range(ref.shape[0]):
        place = jnp.where(ref[i] == value, i, place)
    return place


def panel_kernel(col_map, local, keep, give, buffer, sems):
    n_y, _, slots, thin, size = keep.shape
    core = lax.axis_index("gz") & 1
    copies = []
    for k in range(2):
        first = pl.multiple_of((find(col_map, k) & (slots - 1)) * size, size)
        copies.append(
            pltpu.make_async_copy(local.at[:, pl.ds(first, size)], buffer.at[k], sems.at[k])
        )
        copies[k].start()
    for k in range(2):
        copies[k].wait()
        for p in range(slots):
            for y in range(n_y):
                for out, which in ((keep, core), (give, 1 - core)):
                    first = pl.multiple_of(p * size + y * 2 * thin + which * thin, thin)
                    out[y, k, p] = buffer[k, pl.ds(first, thin), :].astype(jnp.float32)


def cut_panels(col_map, local, slots, n_y, thin, size):
    shape = jax.ShapeDtypeStruct((n_y, 2, slots, thin, size), jnp.float32)
    return pl.pallas_call(
        panel_kernel,
        out_shape=[shape, shape],
        in_specs=[SMEM, pl.BlockSpec(memory_space=pl.ANY)],
        out_specs=[VMEM, VMEM],
        scratch_shapes=[
            pltpu.VMEM((2, local.shape[0], size), jnp.bfloat16),
            pltpu.SemaphoreType.DMA((2,)),
        ],
        compiler_params=PARAMS,
    )(col_map, local)


def give_kernel(where, local, out):
    out[0] = local[...].astype(jnp.float32)


def cut_give(where, local, n_y, width):
    rows = local.shape[0]
    return pl.pallas_call(
        give_kernel,
        out_shape=jax.ShapeDtypeStruct((n_y, rows, width), jnp.float32),
        grid_spec=pltpu.PrefetchScalarGridSpec(
            num_scalar_prefetch=1,
            grid=(n_y,),
            in_specs=[pl.BlockSpec((rows, width), lambda i, w: (0, 2 * i + 1 - w[1]))],
            out_specs=pl.BlockSpec((1, rows, width), lambda i, w: (i, 0, 0)),
        ),
        compiler_params=PARAMS,
    )(where, local)


def add_kernel(where, local, other, *outs):
    for step in range(len(outs)):

        @pl.when(pl.program_id(0) == step)
        def _(out=outs[step]):
            out[...] = local[...].astype(jnp.float32) + other[0]


def add_cores(where, local, other, n_y, width):
    rows = local.shape[0]
    shape = jax.ShapeDtypeStruct((rows, width), jnp.float32)
    return pl.pallas_call(
        add_kernel,
        out_shape=[shape] * n_y,
        grid_spec=pltpu.PrefetchScalarGridSpec(
            num_scalar_prefetch=1,
            grid=(n_y,),
            in_specs=[
                pl.BlockSpec((rows, width), lambda i, w: (0, 2 * ((w[0] + i) & (n_y - 1)) + w[1])),
                pl.BlockSpec((1, rows, width), lambda i, w: ((w[0] + i) & (n_y - 1), 0, 0)),
            ],
            out_specs=[pl.BlockSpec((rows, width), lambda i, w: (0, 0))] * n_y,
        ),
        compiler_params=PARAMS,
    )(where, local, other)


def mask_at(block_pattern, row, col):
    return jnp.where(row == col, 1, block_pattern[row, col]).astype(jnp.float32)


def column_of(col_map, n_y):
    return col_map[lax.axis_index("col") * n_y + (lax.axis_index("gz") >> 1)]


def first_kernel(n_y, block_pattern, col_map, lower_inv, upper_inv, rows, up_out, term_out):
    col = column_of(col_map, n_y)
    mask = jnp.where(col > 0, mask_at(block_pattern, 0, col), 0.0)
    up = mask * mm(lower_inv[0], rows[0])
    up_out[...] = up
    term_out[...] = mm(upper_inv[0], up)


def first_terms(n_y, block_pattern, col_map, lower_inv, upper_inv, rows):
    shape = jax.ShapeDtypeStruct(rows.shape[1:], jnp.float32)
    return pl.pallas_call(
        functools.partial(first_kernel, n_y),
        out_shape=[shape, shape],
        in_specs=[SMEM] * 2 + [VMEM] * 3,
        out_specs=[VMEM, VMEM],
        compiler_params=PARAMS,
    )(block_pattern, col_map, lower_inv, upper_inv, rows)


def last_kernel(n_y, block_pattern, row_map, col_map, lower_inv, upper_inv, rows, up0, term0,
                ring, across, merged, out, high, low):
    slots = high.shape[1] - 1
    size, width = up0.shape
    thin = size // (2 * n_y)
    y = lax.axis_index("gz") >> 1
    core = lax.axis_index("gz") & 1
    col = column_of(col_map, n_y)
    order = [slots] + list(range(slots))
    for p in order:
        for source, which in ((ring, core), (across, 1 - core)):
            for step in range(n_y):
                owner = 2 * ((y + n_y - step) & (n_y - 1)) + which
                first = pl.multiple_of(owner * thin, thin)
                for k in range(2):
                    a, b = halves(source[step, k, p * thin : (p + 1) * thin, :])
                    high[k, p, pl.ds(first, thin), :] = a
                    low[k, p, pl.ds(first, thin), :] = b

    def stored(k, p):
        return high[k, p], low[k, p]

    lower0, lower1 = halves(lower_inv[0]), halves(lower_inv[1])
    upper0, upper1 = halves(upper_inv[0]), halves(upper_inv[1])
    up0 = up0[...]
    low_at = mask_at(block_pattern, 1, 0) * mm_halves(stored(0, slots), upper0)
    up_at = mask_at(block_pattern, 0, 1) * mm_halves(lower0, stored(1, slots))
    mask = jnp.where(col > 1, mask_at(block_pattern, 1, col), 0.0)
    up1 = mask * mm_halves(lower1, halves(rows[1] - mm(low_at, up0)))
    term1 = mm_halves(upper1, halves(up1))

    def own_half(matrix):
        left, right = matrix[:, :width], matrix[:, width:]
        return jnp.where(core == 0, left, right)

    term0 = jnp.where(col == 0, -own_half(upper_inv[0]), term0[...])
    term1 = jnp.where(col == 1, -own_half(upper_inv[1]), term1)
    term2 = mm_halves(upper0, halves(mm(up_at, term1)))
    both = halves(jnp.concatenate([term0, term2], axis=1))
    term1 = halves(term1)
    for p in range(slots):
        row = row_map[lax.axis_index("row") * slots + p]
        own = mask_at(block_pattern, row, col)
        keep0 = jnp.where(row > 0, mask_at(block_pattern, row, 0), 0.0)
        keep1 = jnp.where(row > 1, mask_at(block_pattern, row, 1), 0.0)
        panel0 = (col == 0) & (row > 0)
        panel1 = (col == 1) & (row > 1)
        scale = jnp.where(panel0 | panel1, 0.0, own)
        scale0 = jnp.where(panel0, keep0, scale * keep0)
        scale1 = jnp.where(panel1, keep1, scale * keep1)
        two = mm_halves(stored(0, p), both)
        one = mm_halves(stored(1, p), term1)
        here = slice(p * size, (p + 1) * size)
        value = (
            scale * merged[here, :]
            - scale0 * two[:, :width]
            - scale1 * (one - keep0 * two[:, width:])
        )
        value = jnp.where((row == 0) & (col > 0), up0, value)
        value = jnp.where((row == 1) & (col > 1), up1, value)
        out[here, :] = value.astype(jnp.bfloat16)


def last_terms(n_y, slots, block_pattern, row_map, col_map, lower_inv, upper_inv, rows, up0, term0,
               ring, across, merged):
    size = lower_inv.shape[-1]
    return pl.pallas_call(
        functools.partial(last_kernel, n_y),
        out_shape=jax.ShapeDtypeStruct(merged.shape, jnp.bfloat16),
        in_specs=[SMEM] * 3 + [VMEM] * 8,
        out_specs=VMEM,
        scratch_shapes=[pltpu.VMEM((2, slots + 1, size, size), jnp.bfloat16)] * 2,
        compiler_params=PARAMS,
    )(block_pattern, row_map, col_map, lower_inv, upper_inv, rows, up0, term0, ring, across, merged)


def swap(x, axis, size, bit):
    return lax.ppermute(x, axis, [(i, i ^ bit) for i in range(size)])


def bit_of(index, bit):
    return (index & jnp.uint32(bit)) != 0


def part(x, axis, second):
    half = x.shape[axis] // 2
    return lax.dynamic_slice_in_dim(x, second.astype(jnp.uint32) * half, half, axis)


def join(mine, other, axis, second):
    return jnp.where(
        second,
        jnp.concatenate([other, mine], axis),
        jnp.concatenate([mine, other], axis),
    )


def choose(mine, other, me, sources, bit):
    same = [bit_of(me, bit) == bit_of(s, bit) for s in sources]
    return jnp.stack([jnp.where(same[k], mine[k], other[k]) for k in range(2)])


def pick(x, index, axis):
    return lax.dynamic_index_in_dim(x, index, axis, keepdims=False)


def shards(contributions, block_pattern, row_map, col_map, lower_inv, upper_inv):
    size = upper_inv.shape[-1]
    local = contributions[0]
    slots = local.shape[0] // size
    n_gz, n_row, n_col = lax.axis_size("gz"), lax.axis_size("row"), lax.axis_size("col")
    gz, row, col = [lax.axis_index(a).astype(jnp.uint32) for a in ("gz", "row", "col")]
    y, core = gz >> 1, gz & 1
    n_y = n_gz // 2
    thin = size // n_gz
    width = local.shape[1] // n_gz
    row_at = [position_of(row_map, k) for k in range(2)]
    col_at = [position_of(col_map, k) for k in range(2)]
    shift = slots.bit_length() - 1
    row_owner = [p >> shift for p in row_at]
    col_owner = [p >> shift for p in col_at]
    row_slot = [p & (slots - 1) for p in row_at]
    where = jnp.stack([y, core]).astype(jnp.int32)

    def around(step):
        return [(2 * i + c, 2 * ((i + step) % n_y) + c) for i in range(n_y) for c in range(2)]

    keep, give = cut_panels(col_map, local, slots, n_y, thin, size)
    parts = keep + swap(give, "gz", n_gz, 1)
    panel = pick(parts, y, 0)
    for step in (1, 3, 2):
        chunk = pick(parts, (y + step) & (n_y - 1), 0)
        panel = panel + lax.ppermute(chunk, "gz", around(step))

    other = swap(cut_give(where, local, n_y, width), "gz", n_gz, 1)
    parts = add_cores(where, local, other, n_y, width)
    arrived = [lax.ppermute(parts[step], "gz", around(step)) for step in (1, 3, 2)]

    corner = jnp.stack([pick(panel[k], row_slot[1 - k], 0) for k in range(2)])
    for bit in (2, 4):
        corner = choose(corner, swap(corner, "row", n_row, bit), row, row_owner[::-1], bit)
    mirror = [(r * n_col + c, (r ^ 1) * n_col + c ^ (n_col - 1)) for r in range(n_row) for c in range(n_col)]
    other = lax.ppermute(corner, ("row", "col"), mirror)
    same = [bit_of(row, 1) == bit_of(r, 1) for r in row_owner[::-1]]
    corner = jnp.stack([jnp.where(same[k], corner[k], other[k]) for k in range(2)])
    corner_owner = [jnp.where(same[k], col_owner[k], col_owner[k] ^ (n_col - 1)) for k in range(2)]

    data = panel.reshape(2, slots * thin, size)
    for bit in (1, 2):
        second = bit_of(col, bit)
        other = swap(part(data, 1, ~second), "col", n_col, bit)
        data = choose(part(data, 1, second), other, col, col_owner, bit)
    data, arrived = lax.optimization_barrier((data, arrived))
    merged = parts[0] + (arrived[0] + arrived[1] + arrived[2])
    both = jnp.concatenate([data, corner], 1)
    other = swap(both, "col", n_col, 4)
    thick = data.shape[1]
    data = choose(data, other[:, :thick], col, col_owner, 4)
    corner = choose(corner, other[:, thick:], col, corner_owner, 4)
    for bit in (2, 1):
        second = bit_of(col, bit)
        thick = data.shape[1]
        other = swap(jnp.concatenate([data, corner], 1), "col", n_col, bit)
        data = join(data, other[:, :thick], 1, second)
        corner = choose(corner, other[:, thick:], col, corner_owner, bit)

    mine = jnp.concatenate([data, corner], 1)
    ring = [mine] + [lax.ppermute(mine, "gz", around(step)) for step in (1, 2, 3)]
    ring = jnp.stack(ring)
    across = swap(ring, "gz", n_gz, 1)

    blocks = merged.reshape(slots, size, width)
    rows = jnp.stack([pick(blocks, p, 0) for p in row_slot])
    for bit in (2, 4):
        second = bit_of(row, bit)
        other = swap(part(rows, 1, ~second), "row", n_row, bit)
        rows = choose(part(rows, 1, second), other, row, row_owner, bit)
    rows = choose(rows, swap(rows, "row", n_row, 1), row, row_owner, 1)
    for bit in (4, 2):
        rows = join(rows, swap(rows, "row", n_row, bit), 1, bit_of(row, bit))

    up0, term0 = first_terms(n_y, block_pattern, col_map, lower_inv, upper_inv, rows)
    return last_terms(n_y, slots, block_pattern, row_map, col_map, lower_inv, upper_inv, rows,
                      up0, term0, ring, across, merged)


def solution(mesh):
    in_specs = (P("gz", "row", "col"), P(), P(), P(), P(), P())
    out_specs = P("row", ("col", "gz"))
    return jax.shard_map(shards, mesh=mesh, in_specs=in_specs, out_specs=out_specs, check_vma=False)
```

```python
import functools

import jax
import jax.numpy as jnp
from jax import lax
from jax.experimental import pallas as pl
from jax.experimental.pallas import tpu as pltpu
from jax.sharding import PartitionSpec as P

VMEM = pl.BlockSpec(memory_space=pltpu.VMEM)
SMEM = pl.BlockSpec(memory_space=pltpu.SMEM)
PARAMS = pltpu.CompilerParams(vmem_limit_bytes=32 << 20)


def position_of(table, value):
    iota = jnp.arange(table.shape[0], dtype=jnp.uint32)
    return jnp.sum(jnp.where(table == value, iota, 0), dtype=jnp.uint32)


def halves(a):
    high = a.astype(jnp.bfloat16)
    return high, (a - high.astype(jnp.float32)).astype(jnp.bfloat16)


def mm_halves(a, b):
    dot = functools.partial(jnp.dot, preferred_element_type=jnp.float32)
    return dot(a[0], b[0]) + (dot(a[0], b[1]) + dot(a[1], b[0]))


def mm(a, b):
    return mm_halves(halves(a), halves(b))


def find(ref, value):
    place = jnp.int32(0)
    for i in range(ref.shape[0]):
        place = jnp.where(ref[i] == value, i, place)
    return place


def panel_kernel(col_map, local, keep, give, buffer, sems):
    n_y, _, slots, thin, size = keep.shape
    core = lax.axis_index("gz") & 1
    copies = []
    for k in range(2):
        first = pl.multiple_of((find(col_map, k) & (slots - 1)) * size, size)
        copies.append(
            pltpu.make_async_copy(local.at[:, pl.ds(first, size)], buffer.at[k], sems.at[k])
        )
        copies[k].start()
    for k in range(2):
        copies[k].wait()
        for p in range(slots):
            for y in range(n_y):
                for out, which in ((keep, core), (give, 1 - core)):
                    first = pl.multiple_of(p * size + y * 2 * thin + which * thin, thin)
                    out[y, k, p] = buffer[k, pl.ds(first, thin), :].astype(jnp.float32)


def cut_panels(col_map, local, slots, n_y, thin, size):
    shape = jax.ShapeDtypeStruct((n_y, 2, slots, thin, size), jnp.float32)
    return pl.pallas_call(
        panel_kernel,
        out_shape=[shape, shape],
        in_specs=[SMEM, pl.BlockSpec(memory_space=pl.ANY)],
        out_specs=[VMEM, VMEM],
        scratch_shapes=[
            pltpu.VMEM((2, local.shape[0], size), jnp.bfloat16),
            pltpu.SemaphoreType.DMA((2,)),
        ],
        compiler_params=PARAMS,
    )(col_map, local)


def mask_at(block_pattern, row, col):
    return jnp.where(row == col, 1, block_pattern[row, col]).astype(jnp.float32)


def column_of(col_map, n_y):
    return col_map[lax.axis_index("col") * n_y + (lax.axis_index("gz") >> 1)]


def first_kernel(n_y, block_pattern, col_map, lower_inv, upper_inv, rows, up_out, term_out):
    col = column_of(col_map, n_y)
    mask = jnp.where(col > 0, mask_at(block_pattern, 0, col), 0.0)
    up = mask * mm(lower_inv[0], rows[0])
    up_out[...] = up
    term_out[...] = mm(upper_inv[0], up)


def first_terms(n_y, block_pattern, col_map, lower_inv, upper_inv, rows):
    shape = jax.ShapeDtypeStruct(rows.shape[1:], jnp.float32)
    return pl.pallas_call(
        functools.partial(first_kernel, n_y),
        out_shape=[shape, shape],
        in_specs=[SMEM] * 2 + [VMEM] * 3,
        out_specs=[VMEM, VMEM],
        compiler_params=PARAMS,
    )(block_pattern, col_map, lower_inv, upper_inv, rows)


def last_kernel(n_y, block_pattern, row_map, col_map, lower_inv, upper_inv, rows, up0, term0,
                ring, across, merged, out, high, low):
    slots = high.shape[1] - 1
    size, width = up0.shape
    thin = size // (2 * n_y)
    y = lax.axis_index("gz") >> 1
    core = lax.axis_index("gz") & 1
    col = column_of(col_map, n_y)
    order = [slots] + list(range(slots))
    for p in order:
        for source, which in ((ring, core), (across, 1 - core)):
            for step in range(n_y):
                owner = 2 * ((y + n_y - step) & (n_y - 1)) + which
                first = pl.multiple_of(owner * thin, thin)
                for k in range(2):
                    a, b = halves(source[step, k, p * thin : (p + 1) * thin, :])
                    high[k, p, pl.ds(first, thin), :] = a
                    low[k, p, pl.ds(first, thin), :] = b

    def stored(k, p):
        return high[k, p], low[k, p]

    lower0, lower1 = halves(lower_inv[0]), halves(lower_inv[1])
    upper0, upper1 = halves(upper_inv[0]), halves(upper_inv[1])
    up0 = up0[...]
    low_at = mask_at(block_pattern, 1, 0) * mm_halves(stored(0, slots), upper0)
    up_at = mask_at(block_pattern, 0, 1) * mm_halves(lower0, stored(1, slots))
    mask = jnp.where(col > 1, mask_at(block_pattern, 1, col), 0.0)
    up1 = mask * mm_halves(lower1, halves(rows[1] - mm(low_at, up0)))
    term1 = mm_halves(upper1, halves(up1))

    def own_half(matrix):
        left, right = matrix[:, :width], matrix[:, width:]
        return jnp.where(core == 0, left, right)

    term0 = jnp.where(col == 0, -own_half(upper_inv[0]), term0[...])
    term1 = jnp.where(col == 1, -own_half(upper_inv[1]), term1)
    term2 = mm_halves(upper0, halves(mm(up_at, term1)))
    both = halves(jnp.concatenate([term0, term2], axis=1))
    term1 = halves(term1)
    for p in range(slots):
        row = row_map[lax.axis_index("row") * slots + p]
        own = mask_at(block_pattern, row, col)
        keep0 = jnp.where(row > 0, mask_at(block_pattern, row, 0), 0.0)
        keep1 = jnp.where(row > 1, mask_at(block_pattern, row, 1), 0.0)
        panel0 = (col == 0) & (row > 0)
        panel1 = (col == 1) & (row > 1)
        scale = jnp.where(panel0 | panel1, 0.0, own)
        scale0 = jnp.where(panel0, keep0, scale * keep0)
        scale1 = jnp.where(panel1, keep1, scale * keep1)
        two = mm_halves(stored(0, p), both)
        one = mm_halves(stored(1, p), term1)
        here = slice(p * size, (p + 1) * size)
        value = (
            scale * merged[here, :]
            - scale0 * two[:, :width]
            - scale1 * (one - keep0 * two[:, width:])
        )
        value = jnp.where((row == 0) & (col > 0), up0, value)
        value = jnp.where((row == 1) & (col > 1), up1, value)
        out[here, :] = value.astype(jnp.bfloat16)


def last_terms(n_y, slots, block_pattern, row_map, col_map, lower_inv, upper_inv, rows, up0, term0,
               ring, across, merged):
    size = lower_inv.shape[-1]
    return pl.pallas_call(
        functools.partial(last_kernel, n_y),
        out_shape=jax.ShapeDtypeStruct(merged.shape, jnp.bfloat16),
        in_specs=[SMEM] * 3 + [VMEM] * 8,
        out_specs=VMEM,
        scratch_shapes=[pltpu.VMEM((2, slots + 1, size, size), jnp.bfloat16)] * 2,
        compiler_params=PARAMS,
    )(block_pattern, row_map, col_map, lower_inv, upper_inv, rows, up0, term0, ring, across, merged)


def swap(x, axis, size, bit):
    return lax.ppermute(x, axis, [(i, i ^ bit) for i in range(size)])


def bit_of(index, bit):
    return (index & jnp.uint32(bit)) != 0


def part(x, axis, second):
    half = x.shape[axis] // 2
    return lax.dynamic_slice_in_dim(x, second.astype(jnp.uint32) * half, half, axis)


def join(mine, other, axis, second):
    return jnp.where(
        second,
        jnp.concatenate([other, mine], axis),
        jnp.concatenate([mine, other], axis),
    )


def choose(mine, other, me, sources, bit):
    same = [bit_of(me, bit) == bit_of(s, bit) for s in sources]
    return jnp.stack([jnp.where(same[k], mine[k], other[k]) for k in range(2)])


def pick(x, index, axis):
    return lax.dynamic_index_in_dim(x, index, axis, keepdims=False)


def shards(contributions, block_pattern, row_map, col_map, lower_inv, upper_inv):
    size = upper_inv.shape[-1]
    local = contributions[0]
    slots = local.shape[0] // size
    n_gz, n_row, n_col = lax.axis_size("gz"), lax.axis_size("row"), lax.axis_size("col")
    gz, row, col = [lax.axis_index(a).astype(jnp.uint32) for a in ("gz", "row", "col")]
    y, core = gz >> 1, gz & 1
    n_y = n_gz // 2
    thin = size // n_gz
    width = local.shape[1] // n_gz
    row_at = [position_of(row_map, k) for k in range(2)]
    col_at = [position_of(col_map, k) for k in range(2)]
    shift = slots.bit_length() - 1
    row_owner = [p >> shift for p in row_at]
    col_owner = [p >> shift for p in col_at]
    row_slot = [p & (slots - 1) for p in row_at]
    def around(step):
        return [(2 * i + c, 2 * ((i + step) % n_y) + c) for i in range(n_y) for c in range(2)]

    keep, give = cut_panels(col_map, local, slots, n_y, thin, size)
    parts = keep + swap(give, "gz", n_gz, 1)
    panel = pick(parts, y, 0)
    for step in (1, 3, 2):
        chunk = pick(parts, (y + step) & (n_y - 1), 0)
        panel = panel + lax.ppermute(chunk, "gz", around(step))

    merged = lax.psum_scatter(local.astype(jnp.float32), "gz", scatter_dimension=1, tiled=True)

    corner = jnp.stack([pick(panel[k], row_slot[1 - k], 0) for k in range(2)])
    for bit in (2, 4):
        corner = choose(corner, swap(corner, "row", n_row, bit), row, row_owner[::-1], bit)
    mirror = [(r * n_col + c, (r ^ 1) * n_col + c ^ (n_col - 1)) for r in range(n_row) for c in range(n_col)]
    other = lax.ppermute(corner, ("row", "col"), mirror)
    same = [bit_of(row, 1) == bit_of(r, 1) for r in row_owner[::-1]]
    corner = jnp.stack([jnp.where(same[k], corner[k], other[k]) for k in range(2)])
    corner_owner = [jnp.where(same[k], col_owner[k], col_owner[k] ^ (n_col - 1)) for k in range(2)]

    data = panel.reshape(2, slots * thin, size)
    for bit in (1, 2):
        second = bit_of(col, bit)
        other = swap(part(data, 1, ~second), "col", n_col, bit)
        data = choose(part(data, 1, second), other, col, col_owner, bit)
    data, merged = lax.optimization_barrier((data, merged))
    blocks = merged.reshape(slots, size, width)
    rows = jnp.stack([pick(blocks, p, 0) for p in row_slot])

    def narrow(rows, bit):
        second = bit_of(row, bit)
        other = swap(part(rows, 1, ~second), "row", n_row, bit)
        return choose(part(rows, 1, second), other, row, row_owner, bit)

    def widen(rows, bit):
        return join(rows, swap(rows, "row", n_row, bit), 1, bit_of(row, bit))

    def send_both(data, corner, bit):
        other = swap(jnp.concatenate([data, corner], 1), "col", n_col, bit)
        thick = data.shape[1]
        corner = choose(corner, other[:, thick:], col, corner_owner, bit)
        return other[:, :thick], corner

    other, corner = send_both(data, corner, 4)
    data = choose(data, other, col, col_owner, 4)
    rows = narrow(rows, 2)
    other, corner = send_both(data, corner, 2)
    data = join(data, other, 1, bit_of(col, 2))
    data, rows = lax.optimization_barrier((data, rows))
    rows = narrow(rows, 4)
    other, corner = send_both(data, corner, 1)
    data = join(data, other, 1, bit_of(col, 1))

    mine = jnp.concatenate([data, corner], 1)
    mine, rows = lax.optimization_barrier((mine, rows))
    rows = choose(rows, swap(rows, "row", n_row, 1), row, row_owner, 1)
    rows = widen(rows, 4)
    ring = [mine] + [lax.ppermute(mine, "gz", around(step)) for step in (1, 2, 3)]
    ring = jnp.stack(ring)
    ring, rows = lax.optimization_barrier((ring, rows))
    across = swap(ring, "gz", n_gz, 1)
    rows = widen(rows, 2)

    up0, term0 = first_terms(n_y, block_pattern, col_map, lower_inv, upper_inv, rows)
    return last_terms(n_y, slots, block_pattern, row_map, col_map, lower_inv, upper_inv, rows,
                      up0, term0, ring, across, merged)


def solution(mesh):
    in_specs = (P("gz", "row", "col"), P(), P(), P(), P(), P())
    out_specs = P("row", ("col", "gz"))
    return jax.shard_map(shards, mesh=mesh, in_specs=in_specs, out_specs=out_specs, check_vma=False)
```

```python
import functools

import jax
import jax.numpy as jnp
from jax import lax
from jax.experimental import pallas as pl
from jax.experimental.pallas import tpu as pltpu
from jax.sharding import PartitionSpec as P

VMEM = pl.BlockSpec(memory_space=pltpu.VMEM)
SMEM = pl.BlockSpec(memory_space=pltpu.SMEM)
PARAMS = pltpu.CompilerParams(vmem_limit_bytes=32 << 20)


def position_of(table, value):
    iota = jnp.arange(table.shape[0], dtype=jnp.uint32)
    return jnp.sum(jnp.where(table == value, iota, 0), dtype=jnp.uint32)


def halves(a):
    high = a.astype(jnp.bfloat16)
    return high, (a - high.astype(jnp.float32)).astype(jnp.bfloat16)


def mm_halves(a, b):
    dot = functools.partial(jnp.dot, preferred_element_type=jnp.float32)
    return dot(a[0], b[0]) + (dot(a[0], b[1]) + dot(a[1], b[0]))


def mm(a, b):
    return mm_halves(halves(a), halves(b))


def find(ref, value):
    place = jnp.int32(0)
    for i in range(ref.shape[0]):
        place = jnp.where(ref[i] == value, i, place)
    return place


def panel_kernel(col_map, local, keep, give, buffer, sems):
    n_y, _, slots, thin, size = keep.shape
    core = lax.axis_index("gz") & 1
    copies = []
    for k in range(2):
        first = pl.multiple_of((find(col_map, k) & (slots - 1)) * size, size)
        copies.append(
            pltpu.make_async_copy(local.at[:, pl.ds(first, size)], buffer.at[k], sems.at[k])
        )
        copies[k].start()
    for k in range(2):
        copies[k].wait()
        for p in range(slots):
            for y in range(n_y):
                for out, which in ((keep, core), (give, 1 - core)):
                    first = pl.multiple_of(p * size + y * 2 * thin + which * thin, thin)
                    out[y, k, p] = buffer[k, pl.ds(first, thin), :].astype(jnp.float32)


def cut_panels(col_map, local, slots, n_y, thin, size):
    shape = jax.ShapeDtypeStruct((n_y, 2, slots, thin, size), jnp.float32)
    return pl.pallas_call(
        panel_kernel,
        out_shape=[shape, shape],
        in_specs=[SMEM, pl.BlockSpec(memory_space=pltpu.HBM)],
        out_specs=[VMEM, VMEM],
        scratch_shapes=[
            pltpu.VMEM((2, local.shape[0], size), jnp.bfloat16),
            pltpu.SemaphoreType.DMA((2,)),
        ],
        compiler_params=PARAMS,
    )(col_map, local)


def mask_at(block_pattern, row, col):
    return jnp.where(row == col, 1, block_pattern[row, col]).astype(jnp.float32)


def column_of(col_map, n_y):
    return col_map[lax.axis_index("col") * n_y + (lax.axis_index("gz") >> 1)]


def first_kernel(n_y, block_pattern, col_map, lower_inv, upper_inv, rows, up_out, term_out):
    col = column_of(col_map, n_y)
    mask = jnp.where(col > 0, mask_at(block_pattern, 0, col), 0.0)
    up = mask * mm(lower_inv[0], rows[0])
    up_out[...] = up
    term_out[...] = mm(upper_inv[0], up)


def first_terms(n_y, block_pattern, col_map, lower_inv, upper_inv, rows):
    shape = jax.ShapeDtypeStruct(rows.shape[1:], jnp.float32)
    return pl.pallas_call(
        functools.partial(first_kernel, n_y),
        out_shape=[shape, shape],
        in_specs=[SMEM] * 2 + [VMEM] * 3,
        out_specs=[VMEM, VMEM],
        compiler_params=PARAMS,
    )(block_pattern, col_map, lower_inv, upper_inv, rows)


def last_kernel(n_y, block_pattern, row_map, col_map, lower_inv, upper_inv, rows, up0, term0,
                panels, ring, across, merged, out, high, low):
    slots = high.shape[1] - 1
    size, width = up0.shape
    thin = size // (2 * n_y)
    y = lax.axis_index("gz") >> 1
    core = lax.axis_index("gz") & 1
    col = column_of(col_map, n_y)
    for source, which in ((ring, core), (across, 1 - core)):
        for step in range(n_y):
            owner = 2 * ((y + n_y - step) & (n_y - 1)) + which
            here = pl.ds(pl.multiple_of(owner * thin, thin), thin)
            for k in range(2):
                for half in range(2):
                    lanes = slice(half * width, (half + 1) * width)
                    a, b = halves(source[step, k, half * thin : (half + 1) * thin, :])
                    high[k, slots, here, lanes] = a
                    low[k, slots, here, lanes] = b
    for p in range(slots):
        for owner in range(2 * n_y):
            here = slice(owner * thin, (owner + 1) * thin)
            for k in range(2):
                a, b = halves(panels[owner, k, p * thin : (p + 1) * thin, :])
                high[k, p, here, :] = a
                low[k, p, here, :] = b

    def stored(k, p):
        return high[k, p], low[k, p]

    lower0, lower1 = halves(lower_inv[0]), halves(lower_inv[1])
    upper0, upper1 = halves(upper_inv[0]), halves(upper_inv[1])
    up0 = up0[...]
    low_at = mask_at(block_pattern, 1, 0) * mm_halves(stored(0, slots), upper0)
    up_at = mask_at(block_pattern, 0, 1) * mm_halves(lower0, stored(1, slots))
    mask = jnp.where(col > 1, mask_at(block_pattern, 1, col), 0.0)
    up1 = mask * mm_halves(lower1, halves(rows[1] - mm(low_at, up0)))
    term1 = mm_halves(upper1, halves(up1))

    def own_half(matrix):
        left, right = matrix[:, :width], matrix[:, width:]
        return jnp.where(core == 0, left, right)

    term0 = jnp.where(col == 0, -own_half(upper_inv[0]), term0[...])
    term1 = jnp.where(col == 1, -own_half(upper_inv[1]), term1)
    term2 = mm_halves(upper0, halves(mm(up_at, term1)))
    both = halves(jnp.concatenate([term0, term2], axis=1))
    term1 = halves(term1)
    for p in range(slots):
        row = row_map[lax.axis_index("row") * slots + p]
        own = mask_at(block_pattern, row, col)
        keep0 = jnp.where(row > 0, mask_at(block_pattern, row, 0), 0.0)
        keep1 = jnp.where(row > 1, mask_at(block_pattern, row, 1), 0.0)
        panel0 = (col == 0) & (row > 0)
        panel1 = (col == 1) & (row > 1)
        scale = jnp.where(panel0 | panel1, 0.0, own)
        scale0 = jnp.where(panel0, keep0, scale * keep0)
        scale1 = jnp.where(panel1, keep1, scale * keep1)
        two = mm_halves(stored(0, p), both)
        one = mm_halves(stored(1, p), term1)
        here = slice(p * size, (p + 1) * size)
        value = (
            scale * merged[here, :]
            - scale0 * two[:, :width]
            - scale1 * (one - keep0 * two[:, width:])
        )
        value = jnp.where((row == 0) & (col > 0), up0, value)
        value = jnp.where((row == 1) & (col > 1), up1, value)
        out[here, :] = value.astype(jnp.bfloat16)


def last_terms(n_y, slots, block_pattern, row_map, col_map, lower_inv, upper_inv, rows, up0, term0,
               panels, ring, across, merged):
    size = lower_inv.shape[-1]
    return pl.pallas_call(
        functools.partial(last_kernel, n_y),
        out_shape=jax.ShapeDtypeStruct(merged.shape, jnp.bfloat16),
        in_specs=[SMEM] * 3 + [VMEM] * 9,
        out_specs=VMEM,
        scratch_shapes=[pltpu.VMEM((2, slots + 1, size, size), jnp.bfloat16)] * 2,
        compiler_params=PARAMS,
    )(block_pattern, row_map, col_map, lower_inv, upper_inv, rows, up0, term0, panels, ring, across,
      merged)


def swap(x, axis, size, bit):
    return lax.ppermute(x, axis, [(i, i ^ bit) for i in range(size)])


def bit_of(index, bit):
    return (index & jnp.uint32(bit)) != 0


def part(x, axis, second):
    half = x.shape[axis] // 2
    return lax.dynamic_slice_in_dim(x, second.astype(jnp.uint32) * half, half, axis)


def join(mine, other, axis, second):
    return jnp.where(
        second,
        jnp.concatenate([other, mine], axis),
        jnp.concatenate([mine, other], axis),
    )


def choose(mine, other, me, sources, bit):
    same = [bit_of(me, bit) == bit_of(s, bit) for s in sources]
    return jnp.stack([jnp.where(same[k], mine[k], other[k]) for k in range(2)])


def pick(x, index, axis):
    return lax.dynamic_index_in_dim(x, index, axis, keepdims=False)


def shards(contributions, block_pattern, row_map, col_map, lower_inv, upper_inv):
    size = upper_inv.shape[-1]
    local = contributions[0]
    slots = local.shape[0] // size
    n_gz, n_row, n_col = lax.axis_size("gz"), lax.axis_size("row"), lax.axis_size("col")
    gz, row, col = [lax.axis_index(a).astype(jnp.uint32) for a in ("gz", "row", "col")]
    y, core = gz >> 1, gz & 1
    n_y = n_gz // 2
    thin = size // n_gz
    width = local.shape[1] // n_gz
    row_at = [position_of(row_map, k) for k in range(2)]
    col_at = [position_of(col_map, k) for k in range(2)]
    shift = slots.bit_length() - 1
    row_owner = [p >> shift for p in row_at]
    col_owner = [p >> shift for p in col_at]
    row_slot = [p & (slots - 1) for p in row_at]
    def around(step):
        return [(2 * i + c, 2 * ((i + step) % n_y) + c) for i in range(n_y) for c in range(2)]

    keep, give = cut_panels(col_map, local, slots, n_y, thin, size)

    give, local = lax.optimization_barrier((give, local))
    merged = lax.psum_scatter(local.astype(jnp.float32), "gz", scatter_dimension=1, tiled=True)
    parts = keep + swap(give, "gz", n_gz, 1)
    panel = pick(parts, y, 0)
    for step in (1, 3, 2):
        chunk = pick(parts, (y + step) & (n_y - 1), 0)
        panel = panel + lax.ppermute(chunk, "gz", around(step))

    corner = jnp.stack([pick(panel[k], row_slot[1 - k], 0) for k in range(2)])
    data = panel.reshape(2, slots * thin, size)

    def send_both(data, extra, axis, length, bit):
        other = swap(jnp.concatenate([data, extra], 1), axis, length, bit)
        return other[:, : data.shape[1]], other[:, data.shape[1] :]

    for bit in (1, 2, 4):
        mine = data
        if bit < 4:
            second = bit_of(col, bit)
            mine, data = part(data, 1, second), part(data, 1, ~second)
        other, extra = send_both(data, corner, "col", n_col, bit)
        data = choose(mine, other, col, col_owner, bit)
        corner = choose(corner, extra, col, col_owner, bit)

    blocks = merged.reshape(slots, size, width)
    rows = jnp.stack([pick(blocks, p, 0) for p in row_slot])
    corner_rows = row_owner[::-1]
    corner = jnp.concatenate([corner[..., :width], corner[..., width:]], 1)

    def narrow(rows, corner, bit):
        second = bit_of(row, bit)
        other, extra = send_both(part(rows, 1, ~second), corner, "row", n_row, bit)
        rows = choose(part(rows, 1, second), other, row, row_owner, bit)
        return rows, choose(corner, extra, row, corner_rows, bit)

    def widen(x, axis, length, me, bit):
        return join(x, swap(x, axis, length, bit), 1, bit_of(me, bit))

    rows, corner = narrow(rows, corner, 2)
    data = widen(data, "col", n_col, col, 2)
    data, rows = lax.optimization_barrier((data, rows))
    rows, corner = narrow(rows, corner, 4)
    data = widen(data, "col", n_col, col, 1)
    data, rows = lax.optimization_barrier((data, rows))
    panels = lax.all_gather(data, "gz", axis=0)

    other, extra = send_both(rows, corner, "row", n_row, 1)
    rows = choose(rows, other, row, row_owner, 1)
    corner = choose(corner, extra, row, corner_rows, 1)
    ring = jnp.stack([corner] + [lax.ppermute(corner, "gz", around(step)) for step in (1, 2, 3)])
    rows = widen(rows, "row", n_row, row, 4)
    across = swap(ring, "gz", n_gz, 1)
    rows = widen(rows, "row", n_row, row, 2)

    up0, term0 = first_terms(n_y, block_pattern, col_map, lower_inv, upper_inv, rows)
    return last_terms(n_y, slots, block_pattern, row_map, col_map, lower_inv, upper_inv, rows,
                      up0, term0, panels, ring, across, merged)


def solution(mesh):
    in_specs = (P("gz", "row", "col"), P(), P(), P(), P(), P())
    out_specs = P("row", ("col", "gz"))
    return jax.shard_map(shards, mesh=mesh, in_specs=in_specs, out_specs=out_specs, check_vma=False)
```

```python
import functools

import jax
import jax.numpy as jnp
from jax import lax
from jax.experimental import pallas as pl
from jax.experimental.pallas import tpu as pltpu
from jax.sharding import PartitionSpec as P

VMEM = pl.BlockSpec(memory_space=pltpu.VMEM)
SMEM = pl.BlockSpec(memory_space=pltpu.SMEM)
PARAMS = pltpu.CompilerParams(vmem_limit_bytes=32 << 20)


def position_of(table, value):
    iota = jnp.arange(table.shape[0], dtype=jnp.uint32)
    return jnp.sum(jnp.where(table == value, iota, 0), dtype=jnp.uint32)


def halves(a):
    high = a.astype(jnp.bfloat16)
    return high, (a - high.astype(jnp.float32)).astype(jnp.bfloat16)


def mm_halves(a, b):
    dot = functools.partial(jnp.dot, preferred_element_type=jnp.float32)
    return dot(a[0], b[0]) + (dot(a[0], b[1]) + dot(a[1], b[0]))


def mm(a, b):
    return mm_halves(halves(a), halves(b))


def find(ref, value):
    place = jnp.int32(0)
    for i in range(ref.shape[0]):
        place = jnp.where(ref[i] == value, i, place)
    return place


def panel_kernel(col_map, local, keep, give, buffer, sems):
    n_y, panels, slots, thin, size = keep.shape
    core = lax.axis_index("gz") & 1
    places = [find(col_map, k) for k in range(2)]
    if panels == 1:
        own = lax.axis_index("col") == places[1] // slots
        places = [jnp.where(own, places[1], places[0])]
    copies = []
    for k in range(panels):
        first = pl.multiple_of((places[k] & (slots - 1)) * size, size)
        copies.append(
            pltpu.make_async_copy(local.at[:, pl.ds(first, size)], buffer.at[k], sems.at[k])
        )
        copies[k].start()
    for k in range(panels):
        copies[k].wait()
        for p in range(slots):
            for y in range(n_y):
                for out, which in ((keep, core), (give, 1 - core)):
                    first = pl.multiple_of(p * size + y * 2 * thin + which * thin, thin)
                    out[y, k, p] = buffer[k, pl.ds(first, thin), :].astype(jnp.float32)


def cut_panels(col_map, local, panels, slots, n_y, thin, size):
    shape = jax.ShapeDtypeStruct((n_y, panels, slots, thin, size), jnp.float32)
    return pl.pallas_call(
        panel_kernel,
        out_shape=[shape, shape],
        in_specs=[SMEM, pl.BlockSpec(memory_space=pltpu.HBM)],
        out_specs=[VMEM, VMEM],
        scratch_shapes=[
            pltpu.VMEM((panels, local.shape[0], size), jnp.bfloat16),
            pltpu.SemaphoreType.DMA((panels,)),
        ],
        compiler_params=PARAMS,
    )(col_map, local)


def mask_at(block_pattern, row, col):
    return jnp.where(row == col, 1, block_pattern[row, col]).astype(jnp.float32)


def column_of(col_map, n_y):
    return col_map[lax.axis_index("col") * n_y + (lax.axis_index("gz") >> 1)]


def first_kernel(n_y, block_pattern, col_map, lower_inv, upper_inv, rows, up_out, term_out):
    col = column_of(col_map, n_y)
    mask = jnp.where(col > 0, mask_at(block_pattern, 0, col), 0.0)
    up = mask * mm(lower_inv[0], rows[0])
    up_out[...] = up
    term_out[...] = mm(upper_inv[0], up)


def first_terms(n_y, block_pattern, col_map, lower_inv, upper_inv, rows):
    shape = jax.ShapeDtypeStruct(rows.shape[1:], jnp.float32)
    return pl.pallas_call(
        functools.partial(first_kernel, n_y),
        out_shape=[shape, shape],
        in_specs=[SMEM] * 2 + [VMEM] * 3,
        out_specs=[VMEM, VMEM],
        compiler_params=PARAMS,
    )(block_pattern, col_map, lower_inv, upper_inv, rows)


def last_kernel(n_y, block_pattern, row_map, col_map, lower_inv, upper_inv, rows, up0, term0,
                merged, panels, out, high, low, buffer, sems):
    slots = high.shape[1] - 1
    size, width = up0.shape
    thin = size // (2 * n_y)
    core = lax.axis_index("gz") & 1
    col = column_of(col_map, n_y)
    copies = [
        pltpu.make_async_copy(panels.at[:, :, here, :], buffer.at[:, :, here, :], sems.at[i])
        for i, here in enumerate((pl.ds(slots * thin, thin), pl.ds(0, slots * thin)))
    ]
    for copy in copies:
        copy.start()

    def settle(p):
        for owner in range(2 * n_y):
            here = slice(owner * thin, (owner + 1) * thin)
            for k in range(2):
                a, b = halves(buffer[owner, k, p * thin : (p + 1) * thin, :])
                high[k, p, here, :] = a
                low[k, p, here, :] = b

    copies[0].wait()
    settle(slots)

    def stored(k, p):
        return high[k, p], low[k, p]

    lower0, lower1 = halves(lower_inv[0]), halves(lower_inv[1])
    upper0, upper1 = halves(upper_inv[0]), halves(upper_inv[1])
    up0 = up0[...]
    low_at = mask_at(block_pattern, 1, 0) * mm_halves(stored(0, slots), upper0)
    up_at = mask_at(block_pattern, 0, 1) * mm_halves(lower0, stored(1, slots))
    mask = jnp.where(col > 1, mask_at(block_pattern, 1, col), 0.0)
    up1 = mask * mm_halves(lower1, halves(rows[1] - mm(low_at, up0)))
    term1 = mm_halves(upper1, halves(up1))

    def own_half(matrix):
        left, right = matrix[:, :width], matrix[:, width:]
        return jnp.where(core == 0, left, right)

    term0 = jnp.where(col == 0, -own_half(upper_inv[0]), term0[...])
    term1 = jnp.where(col == 1, -own_half(upper_inv[1]), term1)
    term2 = mm_halves(upper0, halves(mm(up_at, term1)))
    both = halves(jnp.concatenate([term0, term2], axis=1))
    term1 = halves(term1)
    copies[1].wait()
    for p in range(slots):
        settle(p)
        row = row_map[lax.axis_index("row") * slots + p]
        own = mask_at(block_pattern, row, col)
        keep0 = jnp.where(row > 0, mask_at(block_pattern, row, 0), 0.0)
        keep1 = jnp.where(row > 1, mask_at(block_pattern, row, 1), 0.0)
        panel0 = (col == 0) & (row > 0)
        panel1 = (col == 1) & (row > 1)
        scale = jnp.where(panel0 | panel1, 0.0, own)
        scale0 = jnp.where(panel0, keep0, scale * keep0)
        scale1 = jnp.where(panel1, keep1, scale * keep1)
        two = mm_halves(stored(0, p), both)
        one = mm_halves(stored(1, p), term1)
        here = slice(p * size, (p + 1) * size)
        value = (
            scale * merged[here, :]
            - scale0 * two[:, :width]
            - scale1 * (one - keep0 * two[:, width:])
        )
        value = jnp.where((row == 0) & (col > 0), up0, value)
        value = jnp.where((row == 1) & (col > 1), up1, value)
        out[here, :] = value.astype(jnp.bfloat16)


def last_terms(n_y, slots, block_pattern, row_map, col_map, lower_inv, upper_inv, rows, up0, term0,
               panels, merged):
    size = lower_inv.shape[-1]
    return pl.pallas_call(
        functools.partial(last_kernel, n_y),
        out_shape=jax.ShapeDtypeStruct(merged.shape, jnp.bfloat16),
        in_specs=[SMEM] * 3 + [VMEM] * 6 + [pl.BlockSpec(memory_space=pltpu.HBM)],
        out_specs=VMEM,
        scratch_shapes=[
            pltpu.VMEM((2, slots + 1, size, size), jnp.bfloat16),
            pltpu.VMEM((2, slots + 1, size, size), jnp.bfloat16),
            pltpu.VMEM(panels.shape, jnp.float32),
            pltpu.SemaphoreType.DMA((2,)),
        ],
        compiler_params=PARAMS,
    )(block_pattern, row_map, col_map, lower_inv, upper_inv, rows, up0, term0, merged, panels)


def swap(x, axis, size, bit):
    return lax.ppermute(x, axis, [(i, i ^ bit) for i in range(size)])


def bit_of(index, bit):
    return (index & jnp.uint32(bit)) != 0


def part(x, axis, second):
    half = x.shape[axis] // 2
    return lax.dynamic_slice_in_dim(x, second.astype(jnp.uint32) * half, half, axis)


def join(mine, other, axis, second):
    return jnp.where(
        second,
        jnp.concatenate([other, mine], axis),
        jnp.concatenate([mine, other], axis),
    )


def choose(mine, other, me, sources, bit):
    same = [bit_of(me, bit) == bit_of(s, bit) for s in sources]
    return jnp.stack([jnp.where(same[k], mine[k], other[k]) for k in range(len(sources))])


def pick(x, index, axis):
    return lax.dynamic_index_in_dim(x, index, axis, keepdims=False)


def shards(contributions, block_pattern, row_map, col_map, lower_inv, upper_inv):
    size = upper_inv.shape[-1]
    local = contributions[0]
    slots = local.shape[0] // size
    n_gz, n_row, n_col = lax.axis_size("gz"), lax.axis_size("row"), lax.axis_size("col")
    gz, row, col = [lax.axis_index(a).astype(jnp.uint32) for a in ("gz", "row", "col")]
    y, core = gz >> 1, gz & 1
    n_y = n_gz // 2
    thin = size // n_gz
    width = local.shape[1] // n_gz
    row_at = [position_of(row_map, k) for k in range(2)]
    col_at = [position_of(col_map, k) for k in range(2)]
    shift = slots.bit_length() - 1
    row_owner = [p >> shift for p in row_at]
    col_owner = [p >> shift for p in col_at]
    row_slot = [p & (slots - 1) for p in row_at]
    def around(step):
        return [(2 * i + c, 2 * ((i + step) % n_y) + c) for i in range(n_y) for c in range(2)]

    merged = lax.psum_scatter(local.astype(jnp.float32), "gz", scatter_dimension=1, tiled=True)

    mirror = [
        (r * n_col + c, (r ^ 1) * n_col + c ^ (n_col - 1))
        for r in range(n_row)
        for c in range(n_col)
    ]
    corner_rows = row_owner[::-1]
    same_half = [bit_of(row, 1) == bit_of(r, 1) for r in corner_rows]

    def gather(panels):
        keep, give = cut_panels(col_map, local, panels, slots, n_y, thin, size)
        parts = keep + swap(give, "gz", n_gz, 1)
        panel = pick(parts, y, 0)
        for step in (1, 3, 2):
            chunk = pick(parts, (y + step) & (n_y - 1), 0)
            panel = panel + lax.ppermute(chunk, "gz", around(step))
        if panels == 1:
            second = col == col_owner[1]
            sources = [jnp.where(second, corner_rows[1], corner_rows[0])]
            at = [jnp.where(second, row_slot[0], row_slot[1])]
        else:
            sources, at = corner_rows, row_slot[::-1]
        corner = jnp.stack([pick(panel[k], at[k], 0) for k in range(panels)])
        for bit in (2, 4):
            other = swap(corner, "row", n_row, bit)
            corner = choose(corner, other, row, sources, bit)
        other = lax.ppermute(corner, ("row", "col"), mirror)
        corner = jnp.stack(
            [jnp.where(same_half[k], corner[k % panels], other[k % panels]) for k in range(2)]
        )
        data = panel.reshape(panels, slots * thin, size)
        if panels == 1:
            data = jnp.concatenate([data, data])
        for bit in (1, 2):
            second = bit_of(col, bit)
            other = swap(part(data, 1, ~second), "col", n_col, bit)
            data = choose(part(data, 1, second), other, col, col_owner, bit)
        return data, corner

    data, corner = lax.cond(
        col_owner[0] == col_owner[1], lambda: gather(2), lambda: gather(1)
    )
    corner_owner = [
        jnp.where(same_half[k], col_owner[k], col_owner[k] ^ (n_col - 1)) for k in range(2)
    ]

    blocks = merged.reshape(slots, size, width)
    rows = jnp.stack([pick(blocks, p, 0) for p in row_slot])

    def narrow(rows, bit):
        second = bit_of(row, bit)
        other = swap(part(rows, 1, ~second), "row", n_row, bit)
        return choose(part(rows, 1, second), other, row, row_owner, bit)

    def widen(x, other, me, bit):
        return join(x, other, 1, bit_of(me, bit))

    def send_both(data, corner, bit):
        other = swap(jnp.concatenate([data, corner], 1), "col", n_col, bit)
        thick = data.shape[1]
        return other[:, :thick], choose(corner, other[:, thick:], col, corner_owner, bit)

    other, corner = send_both(data, corner, 4)
    data = choose(data, other, col, col_owner, 4)
    rows = narrow(rows, 2)
    other, corner = send_both(data, corner, 2)
    data = widen(data, other, col, 2)
    data, rows = lax.optimization_barrier((data, rows))
    rows = narrow(rows, 4)
    other, corner = send_both(data, corner, 1)
    data = jnp.concatenate([widen(data, other, col, 1), corner], 1)
    data, rows = lax.optimization_barrier((data, rows))
    panels = lax.all_gather(data, "gz", axis=0)
    rows = choose(rows, swap(rows, "row", n_row, 1), row, row_owner, 1)
    for bit in (4, 2):
        rows = widen(rows, swap(rows, "row", n_row, bit), row, bit)

    up0, term0 = first_terms(n_y, block_pattern, col_map, lower_inv, upper_inv, rows)
    return last_terms(n_y, slots, block_pattern, row_map, col_map, lower_inv, upper_inv, rows,
                      up0, term0, panels, merged)


def solution(mesh):
    in_specs = (P("gz", "row", "col"), P(), P(), P(), P(), P())
    out_specs = P("row", ("col", "gz"))
    return jax.shard_map(shards, mesh=mesh, in_specs=in_specs, out_specs=out_specs, check_vma=False)
```

```python
import functools

import jax
import jax.numpy as jnp
from jax import lax
from jax.experimental import pallas as pl
from jax.experimental.pallas import tpu as pltpu
from jax.sharding import PartitionSpec as P

VMEM = pl.BlockSpec(memory_space=pltpu.VMEM)
SMEM = pl.BlockSpec(memory_space=pltpu.SMEM)
PARAMS = pltpu.CompilerParams(vmem_limit_bytes=32 << 20)
LARGE = pltpu.CompilerParams(vmem_limit_bytes=60 << 20)


def position_of(table, value):
    iota = jnp.arange(table.shape[0], dtype=jnp.uint32)
    return jnp.sum(jnp.where(table == value, iota, 0), dtype=jnp.uint32)


def halves(a):
    high = a.astype(jnp.bfloat16)
    return high, (a - high.astype(jnp.float32)).astype(jnp.bfloat16)


def mm_halves(a, b):
    dot = functools.partial(jnp.dot, preferred_element_type=jnp.float32)
    return dot(a[0], b[0]) + (dot(a[0], b[1]) + dot(a[1], b[0]))


def mm(a, b):
    return mm_halves(halves(a), halves(b))


def find(ref, value):
    place = jnp.int32(0)
    for i in range(ref.shape[0]):
        place = jnp.where(ref[i] == value, i, place)
    return place


def panel_kernel(col_map, local, keep, give, buffer, sems):
    n_y, _, slots, thin, size = keep.shape
    core = lax.axis_index("gz") & 1
    copies = []
    for k in range(2):
        first = pl.multiple_of((find(col_map, k) & (slots - 1)) * size, size)
        copies.append(
            pltpu.make_async_copy(local.at[:, pl.ds(first, size)], buffer.at[k], sems.at[k])
        )
        copies[k].start()
    for k in range(2):
        copies[k].wait()
        for p in range(slots):
            for y in range(n_y):
                for out, which in ((keep, core), (give, 1 - core)):
                    first = pl.multiple_of(p * size + y * 2 * thin + which * thin, thin)
                    out[y, k, p] = buffer[k, pl.ds(first, thin), :].astype(jnp.float32)


def cut_panels(col_map, local, slots, n_y, thin, size):
    shape = jax.ShapeDtypeStruct((n_y, 2, slots, thin, size), jnp.float32)
    return pl.pallas_call(
        panel_kernel,
        out_shape=[shape, shape],
        in_specs=[SMEM, pl.BlockSpec(memory_space=pltpu.HBM)],
        out_specs=[VMEM, VMEM],
        scratch_shapes=[
            pltpu.VMEM((2, local.shape[0], size), jnp.bfloat16),
            pltpu.SemaphoreType.DMA((2,)),
        ],
        compiler_params=LARGE,
    )(col_map, local)


def mask_at(block_pattern, row, col):
    return jnp.where(row == col, 1, block_pattern[row, col]).astype(jnp.float32)


def column_of(col_map, n_y):
    return col_map[lax.axis_index("col") * n_y + (lax.axis_index("gz") >> 1)]


def first_kernel(n_y, block_pattern, col_map, lower_inv, upper_inv, rows, up_out, term_out):
    col = column_of(col_map, n_y)
    mask = jnp.where(col > 0, mask_at(block_pattern, 0, col), 0.0)
    up = mask * mm(lower_inv[0], rows[0])
    up_out[...] = up
    term_out[...] = mm(upper_inv[0], up)


def first_terms(n_y, block_pattern, col_map, lower_inv, upper_inv, rows):
    shape = jax.ShapeDtypeStruct(rows.shape[1:], jnp.float32)
    return pl.pallas_call(
        functools.partial(first_kernel, n_y),
        out_shape=[shape, shape],
        in_specs=[SMEM] * 2 + [VMEM] * 3,
        out_specs=[VMEM, VMEM],
        compiler_params=PARAMS,
    )(block_pattern, col_map, lower_inv, upper_inv, rows)


def last_kernel(n_y, block_pattern, row_map, col_map, lower_inv, upper_inv, rows, up0, term0,
                merged, panels, out, high, low, buffer, sems):
    slots = high.shape[1] - 1
    size, width = up0.shape
    thin = size // (2 * n_y)
    core = lax.axis_index("gz") & 1
    col = column_of(col_map, n_y)
    copies = [
        pltpu.make_async_copy(panels.at[:, :, here, :], buffer.at[:, :, here, :], sems.at[i])
        for i, here in enumerate((pl.ds(slots * thin, thin), pl.ds(0, slots * thin)))
    ]
    for copy in copies:
        copy.start()

    def settle(p):
        for owner in range(2 * n_y):
            here = slice(owner * thin, (owner + 1) * thin)
            for k in range(2):
                a, b = halves(buffer[owner, k, p * thin : (p + 1) * thin, :])
                high[k, p, here, :] = a
                low[k, p, here, :] = b

    copies[0].wait()
    settle(slots)

    def stored(k, p):
        return high[k, p], low[k, p]

    lower0, lower1 = halves(lower_inv[0]), halves(lower_inv[1])
    upper0, upper1 = halves(upper_inv[0]), halves(upper_inv[1])
    up0 = up0[...]
    low_at = mask_at(block_pattern, 1, 0) * mm_halves(stored(0, slots), upper0)
    up_at = mask_at(block_pattern, 0, 1) * mm_halves(lower0, stored(1, slots))
    mask = jnp.where(col > 1, mask_at(block_pattern, 1, col), 0.0)
    up1 = mask * mm_halves(lower1, halves(rows[1] - mm(low_at, up0)))
    term1 = mm_halves(upper1, halves(up1))

    def own_half(matrix):
        left, right = matrix[:, :width], matrix[:, width:]
        return jnp.where(core == 0, left, right)

    term0 = jnp.where(col == 0, -own_half(upper_inv[0]), term0[...])
    term1 = jnp.where(col == 1, -own_half(upper_inv[1]), term1)
    term2 = mm_halves(upper0, halves(mm(up_at, term1)))
    both = halves(jnp.concatenate([term0, term2], axis=1))
    term1 = halves(term1)
    copies[1].wait()
    for p in range(slots):
        settle(p)
        row = row_map[lax.axis_index("row") * slots + p]
        own = mask_at(block_pattern, row, col)
        keep0 = jnp.where(row > 0, mask_at(block_pattern, row, 0), 0.0)
        keep1 = jnp.where(row > 1, mask_at(block_pattern, row, 1), 0.0)
        panel0 = (col == 0) & (row > 0)
        panel1 = (col == 1) & (row > 1)
        scale = jnp.where(panel0 | panel1, 0.0, own)
        scale0 = jnp.where(panel0, keep0, scale * keep0)
        scale1 = jnp.where(panel1, keep1, scale * keep1)
        two = mm_halves(stored(0, p), both)
        one = mm_halves(stored(1, p), term1)
        here = slice(p * size, (p + 1) * size)
        value = (
            scale * merged[here, :]
            - scale0 * two[:, :width]
            - scale1 * (one - keep0 * two[:, width:])
        )
        value = jnp.where((row == 0) & (col > 0), up0, value)
        value = jnp.where((row == 1) & (col > 1), up1, value)
        out[here, :] = value.astype(jnp.bfloat16)


def last_terms(n_y, slots, block_pattern, row_map, col_map, lower_inv, upper_inv, rows, up0, term0,
               panels, merged):
    size = lower_inv.shape[-1]
    return pl.pallas_call(
        functools.partial(last_kernel, n_y),
        out_shape=jax.ShapeDtypeStruct(merged.shape, jnp.bfloat16),
        in_specs=[SMEM] * 3 + [VMEM] * 6 + [pl.BlockSpec(memory_space=pltpu.HBM)],
        out_specs=VMEM,
        scratch_shapes=[
            pltpu.VMEM((2, slots + 1, size, size), jnp.bfloat16),
            pltpu.VMEM((2, slots + 1, size, size), jnp.bfloat16),
            pltpu.VMEM(panels.shape, jnp.float32),
            pltpu.SemaphoreType.DMA((2,)),
        ],
        compiler_params=LARGE,
    )(block_pattern, row_map, col_map, lower_inv, upper_inv, rows, up0, term0, merged, panels)


def swap(x, axis, size, bit):
    return lax.ppermute(x, axis, [(i, i ^ bit) for i in range(size)])


def bit_of(index, bit):
    return (index & jnp.uint32(bit)) != 0


def part(x, axis, second):
    half = x.shape[axis] // 2
    return lax.dynamic_slice_in_dim(x, second.astype(jnp.uint32) * half, half, axis)


def join(mine, other, axis, second):
    return jnp.where(
        second,
        jnp.concatenate([other, mine], axis),
        jnp.concatenate([mine, other], axis),
    )


def choose(mine, other, me, sources, bit):
    same = [bit_of(me, bit) == bit_of(s, bit) for s in sources]
    return jnp.stack([jnp.where(same[k], mine[k], other[k]) for k in range(len(sources))])


def pick(x, index, axis):
    return lax.dynamic_index_in_dim(x, index, axis, keepdims=False)


def shards(contributions, block_pattern, row_map, col_map, lower_inv, upper_inv):
    size = upper_inv.shape[-1]
    local = contributions[0]
    slots = local.shape[0] // size
    n_gz, n_row, n_col = lax.axis_size("gz"), lax.axis_size("row"), lax.axis_size("col")
    gz, row, col = [lax.axis_index(a).astype(jnp.uint32) for a in ("gz", "row", "col")]
    y, core = gz >> 1, gz & 1
    n_y = n_gz // 2
    thin = size // n_gz
    width = local.shape[1] // n_gz
    row_at = [position_of(row_map, k) for k in range(2)]
    col_at = [position_of(col_map, k) for k in range(2)]
    shift = slots.bit_length() - 1
    row_owner = [p >> shift for p in row_at]
    col_owner = [p >> shift for p in col_at]
    row_slot = [p & (slots - 1) for p in row_at]
    def around(step):
        return [(2 * i + c, 2 * ((i + step) % n_y) + c) for i in range(n_y) for c in range(2)]

    keep, give = cut_panels(col_map, local, slots, n_y, thin, size)
    other = swap(give, "gz", n_gz, 1)
    other, local = lax.optimization_barrier((other, local))
    parts = keep + other
    panel = pick(parts, y, 0)
    for step in (1, 3, 2):
        chunk = pick(parts, (y + step) & (n_y - 1), 0)
        panel = panel + lax.ppermute(chunk, "gz", around(step))

    merged = lax.psum_scatter(local.astype(jnp.float32), "gz", scatter_dimension=1, tiled=True)

    corner_rows = row_owner[::-1]
    corner = jnp.stack([pick(panel[k], row_slot[1 - k], 0) for k in range(2)])
    for bit in (2, 4):
        corner = choose(corner, swap(corner, "row", n_row, bit), row, corner_rows, bit)
    mirror = [
        (r * n_col + c, (r ^ 1) * n_col + c ^ (n_col - 1))
        for r in range(n_row)
        for c in range(n_col)
    ]
    corner_other = lax.ppermute(corner, ("row", "col"), mirror)
    corner = choose(corner, corner_other, row, corner_rows, 1)
    corner_owner = [
        jnp.where(bit_of(row, 1) == bit_of(corner_rows[k], 1), c, c ^ (n_col - 1))
        for k, c in enumerate(col_owner)
    ]

    data = panel.reshape(2, slots * thin, size)
    for bit in (1, 2, 4):
        mine = data
        if bit < 4:
            second = bit_of(col, bit)
            mine, data = part(data, 1, second), part(data, 1, ~second)
        data = choose(mine, swap(data, "col", n_col, bit), col, col_owner, bit)
    corner = choose(corner, swap(corner, "col", n_col, 4), col, corner_owner, 4)

    blocks = merged.reshape(slots, size, width)
    rows = jnp.stack([pick(blocks, p, 0) for p in row_slot])

    def narrow(rows, bit):
        second = bit_of(row, bit)
        other = swap(part(rows, 1, ~second), "row", n_row, bit)
        return choose(part(rows, 1, second), other, row, row_owner, bit)

    def widen(x, other, me, bit):
        return join(x, other, 1, bit_of(me, bit))

    def send_both(data, corner, bit):
        other = swap(jnp.concatenate([data, corner], 1), "col", n_col, bit)
        thick = data.shape[1]
        return other[:, :thick], choose(corner, other[:, thick:], col, corner_owner, bit)

    rows = narrow(rows, 2)
    other, corner = send_both(data, corner, 2)
    data = widen(data, other, col, 2)
    data, rows = lax.optimization_barrier((data, rows))
    rows = narrow(rows, 4)
    other, corner = send_both(data, corner, 1)
    data = jnp.concatenate([widen(data, other, col, 1), corner], 1)
    data, rows = lax.optimization_barrier((data, rows))
    panels = lax.all_gather(data, "gz", axis=0)
    rows = choose(rows, swap(rows, "row", n_row, 1), row, row_owner, 1)
    for bit in (4, 2):
        rows = widen(rows, swap(rows, "row", n_row, bit), row, bit)

    up0, term0 = first_terms(n_y, block_pattern, col_map, lower_inv, upper_inv, rows)
    return last_terms(n_y, slots, block_pattern, row_map, col_map, lower_inv, upper_inv, rows,
                      up0, term0, panels, merged)


def solution(mesh):
    in_specs = (P("gz", "row", "col"), P(), P(), P(), P(), P())
    out_specs = P("row", ("col", "gz"))
    return jax.shard_map(shards, mesh=mesh, in_specs=in_specs, out_specs=out_specs, check_vma=False)
```

```python
import functools

import jax
import jax.numpy as jnp
from jax import lax
from jax.experimental import pallas as pl
from jax.experimental.pallas import tpu as pltpu
from jax.sharding import PartitionSpec as P

VMEM = pl.BlockSpec(memory_space=pltpu.VMEM)
SMEM = pl.BlockSpec(memory_space=pltpu.SMEM)
PARAMS = pltpu.CompilerParams(vmem_limit_bytes=32 << 20)
LARGE = pltpu.CompilerParams(vmem_limit_bytes=60 << 20)


def position_of(table, value):
    iota = jnp.arange(table.shape[0], dtype=jnp.uint32)
    return jnp.sum(jnp.where(table == value, iota, 0), dtype=jnp.uint32)


def halves(a):
    high = a.astype(jnp.bfloat16)
    return high, (a - high.astype(jnp.float32)).astype(jnp.bfloat16)


def mm_halves(a, b):
    dot = functools.partial(jnp.dot, preferred_element_type=jnp.float32)
    return dot(a[0], b[0]) + (dot(a[0], b[1]) + dot(a[1], b[0]))


def mm(a, b):
    return mm_halves(halves(a), halves(b))


def find(ref, value):
    place = jnp.int32(0)
    for i in range(ref.shape[0]):
        place = jnp.where(ref[i] == value, i, place)
    return place


def panel_kernel(col_map, local, keep, give, buffer, sems):
    n_y, _, slots, thin, size = keep.shape
    core = lax.axis_index("gz") & 1
    copies = []
    for k in range(2):
        first = pl.multiple_of((find(col_map, k) & (slots - 1)) * size, size)
        copies.append(
            pltpu.make_async_copy(local.at[:, pl.ds(first, size)], buffer.at[k], sems.at[k])
        )
        copies[k].start()
    for k in range(2):
        copies[k].wait()
        for p in range(slots):
            for y in range(n_y):
                for out, which in ((keep, core), (give, 1 - core)):
                    first = pl.multiple_of(p * size + y * 2 * thin + which * thin, thin)
                    out[y, k, p] = buffer[k, pl.ds(first, thin), :].astype(jnp.float32)


def cut_panels(col_map, local, slots, n_y, thin, size):
    shape = jax.ShapeDtypeStruct((n_y, 2, slots, thin, size), jnp.float32)
    return pl.pallas_call(
        panel_kernel,
        out_shape=[shape, shape],
        in_specs=[SMEM, pl.BlockSpec(memory_space=pltpu.HBM)],
        out_specs=[VMEM, VMEM],
        scratch_shapes=[
            pltpu.VMEM((2, local.shape[0], size), jnp.bfloat16),
            pltpu.SemaphoreType.DMA((2,)),
        ],
        compiler_params=PARAMS,
    )(col_map, local)


def mask_at(block_pattern, row, col):
    return jnp.where(row == col, 1, block_pattern[row, col]).astype(jnp.float32)


def column_of(col_map, n_y):
    return col_map[lax.axis_index("col") * n_y + (lax.axis_index("gz") >> 1)]


def first_kernel(n_y, block_pattern, col_map, lower_inv, upper_inv, rows, up_out, term_out):
    col = column_of(col_map, n_y)
    mask = jnp.where(col > 0, mask_at(block_pattern, 0, col), 0.0)
    up = mask * mm(lower_inv[0], rows[0])
    up_out[...] = up
    term_out[...] = mm(upper_inv[0], up)


def first_terms(n_y, block_pattern, col_map, lower_inv, upper_inv, rows):
    shape = jax.ShapeDtypeStruct(rows.shape[1:], jnp.float32)
    return pl.pallas_call(
        functools.partial(first_kernel, n_y),
        out_shape=[shape, shape],
        in_specs=[SMEM] * 2 + [VMEM] * 3,
        out_specs=[VMEM, VMEM],
        compiler_params=PARAMS,
    )(block_pattern, col_map, lower_inv, upper_inv, rows)


def last_kernel(n_y, block_pattern, row_map, col_map, lower_inv, upper_inv, rows, up0, term0,
                merged, panels, out, high, low, buffer, sems):
    slots = high.shape[1] - 1
    size, width = up0.shape
    thin = size // (2 * n_y)
    core = lax.axis_index("gz") & 1
    col = column_of(col_map, n_y)
    copies = [
        pltpu.make_async_copy(panels.at[:, :, here, :], buffer.at[:, :, here, :], sems.at[i])
        for i, here in enumerate((pl.ds(slots * thin, thin), pl.ds(0, slots * thin)))
    ]
    for copy in copies:
        copy.start()

    def settle(p):
        for owner in range(2 * n_y):
            here = slice(owner * thin, (owner + 1) * thin)
            for k in range(2):
                a, b = halves(buffer[owner, k, p * thin : (p + 1) * thin, :])
                high[k, p, here, :] = a
                low[k, p, here, :] = b

    copies[0].wait()
    settle(slots)

    def stored(k, p):
        return high[k, p], low[k, p]

    lower0, lower1 = halves(lower_inv[0]), halves(lower_inv[1])
    upper0, upper1 = halves(upper_inv[0]), halves(upper_inv[1])
    up0 = up0[...]
    low_at = mask_at(block_pattern, 1, 0) * mm_halves(stored(0, slots), upper0)
    up_at = mask_at(block_pattern, 0, 1) * mm_halves(lower0, stored(1, slots))
    mask = jnp.where(col > 1, mask_at(block_pattern, 1, col), 0.0)
    up1 = mask * mm_halves(lower1, halves(rows[1] - mm(low_at, up0)))
    term1 = mm_halves(upper1, halves(up1))

    def own_half(matrix):
        left, right = matrix[:, :width], matrix[:, width:]
        return jnp.where(core == 0, left, right)

    term0 = jnp.where(col == 0, -own_half(upper_inv[0]), term0[...])
    term1 = jnp.where(col == 1, -own_half(upper_inv[1]), term1)
    term2 = mm_halves(upper0, halves(mm(up_at, term1)))
    both = halves(jnp.concatenate([term0, term2], axis=1))
    term1 = halves(term1)
    copies[1].wait()
    for p in range(slots):
        settle(p)
        row = row_map[lax.axis_index("row") * slots + p]
        own = mask_at(block_pattern, row, col)
        keep0 = jnp.where(row > 0, mask_at(block_pattern, row, 0), 0.0)
        keep1 = jnp.where(row > 1, mask_at(block_pattern, row, 1), 0.0)
        panel0 = (col == 0) & (row > 0)
        panel1 = (col == 1) & (row > 1)
        scale = jnp.where(panel0 | panel1, 0.0, own)
        scale0 = jnp.where(panel0, keep0, scale * keep0)
        scale1 = jnp.where(panel1, keep1, scale * keep1)
        two = mm_halves(stored(0, p), both)
        one = mm_halves(stored(1, p), term1)
        here = slice(p * size, (p + 1) * size)
        value = (
            scale * merged[here, :]
            - scale0 * two[:, :width]
            - scale1 * (one - keep0 * two[:, width:])
        )
        value = jnp.where((row == 0) & (col > 0), up0, value)
        value = jnp.where((row == 1) & (col > 1), up1, value)
        out[here, :] = value.astype(jnp.bfloat16)


def last_terms(n_y, slots, block_pattern, row_map, col_map, lower_inv, upper_inv, rows, up0, term0,
               panels, merged):
    size = lower_inv.shape[-1]
    return pl.pallas_call(
        functools.partial(last_kernel, n_y),
        out_shape=jax.ShapeDtypeStruct(merged.shape, jnp.bfloat16),
        in_specs=[SMEM] * 3 + [VMEM] * 6 + [pl.BlockSpec(memory_space=pltpu.HBM)],
        out_specs=VMEM,
        scratch_shapes=[
            pltpu.VMEM((2, slots + 1, size, size), jnp.bfloat16),
            pltpu.VMEM((2, slots + 1, size, size), jnp.bfloat16),
            pltpu.VMEM(panels.shape, jnp.float32),
            pltpu.SemaphoreType.DMA((2,)),
        ],
        compiler_params=LARGE,
    )(block_pattern, row_map, col_map, lower_inv, upper_inv, rows, up0, term0, merged, panels)


def swap(x, axis, size, bit):
    return lax.ppermute(x, axis, [(i, i ^ bit) for i in range(size)])


def bit_of(index, bit):
    return (index & jnp.uint32(bit)) != 0


def part(x, axis, second):
    half = x.shape[axis] // 2
    return lax.dynamic_slice_in_dim(x, second.astype(jnp.uint32) * half, half, axis)


def join(mine, other, axis, second):
    return jnp.where(
        second,
        jnp.concatenate([other, mine], axis),
        jnp.concatenate([mine, other], axis),
    )


def choose(mine, other, me, sources, bit):
    same = [bit_of(me, bit) == bit_of(s, bit) for s in sources]
    return jnp.stack([jnp.where(same[k], mine[k], other[k]) for k in range(len(sources))])


def pick(x, index, axis):
    return lax.dynamic_index_in_dim(x, index, axis, keepdims=False)


def shards(contributions, block_pattern, row_map, col_map, lower_inv, upper_inv):
    size = upper_inv.shape[-1]
    local = contributions[0]
    slots = local.shape[0] // size
    n_gz, n_row, n_col = lax.axis_size("gz"), lax.axis_size("row"), lax.axis_size("col")
    gz, row, col = [lax.axis_index(a).astype(jnp.uint32) for a in ("gz", "row", "col")]
    y, core = gz >> 1, gz & 1
    n_y = n_gz // 2
    thin = size // n_gz
    width = local.shape[1] // n_gz
    row_at = [position_of(row_map, k) for k in range(2)]
    col_at = [position_of(col_map, k) for k in range(2)]
    shift = slots.bit_length() - 1
    row_owner = [p >> shift for p in row_at]
    col_owner = [p >> shift for p in col_at]
    row_slot = [p & (slots - 1) for p in row_at]
    def around(step):
        return [(2 * i + c, 2 * ((i + step) % n_y) + c) for i in range(n_y) for c in range(2)]

    keep, give = cut_panels(col_map, local, slots, n_y, thin, size)
    other = swap(give, "gz", n_gz, 1)
    other, local = lax.optimization_barrier((other, local))
    parts = keep + other
    arrived = [
        lax.ppermute(pick(parts, (y + step) & (n_y - 1), 0), "gz", around(step))
        for step in (1, 3, 2)
    ]
    panel = pick(parts, y, 0) + (arrived[0] + arrived[1] + arrived[2])

    merged = lax.psum_scatter(local.astype(jnp.float32), "gz", scatter_dimension=1, tiled=True)

    corner = jnp.stack([pick(panel[k], row_slot[1 - k], 0) for k in range(2)])
    data = panel.reshape(2, slots * thin, size)

    def send_both(data, extra, axis, length, bit):
        other = swap(jnp.concatenate([data, extra], 1), axis, length, bit)
        return other[:, : data.shape[1]], other[:, data.shape[1] :]

    for bit in (1, 2, 4):
        mine = data
        if bit < 4:
            second = bit_of(col, bit)
            mine, data = part(data, 1, second), part(data, 1, ~second)
        other, extra = send_both(data, corner, "col", n_col, bit)
        data = choose(mine, other, col, col_owner, bit)
        corner = choose(corner, extra, col, col_owner, bit)

    corner_rows = row_owner[::-1]
    mirror = [
        (r * n_col + c, (r ^ 1) * n_col + c ^ (n_col - 1))
        for r in range(n_row)
        for c in range(n_col)
    ]
    corner = choose(corner, lax.ppermute(corner, ("row", "col"), mirror), row, corner_rows, 1)

    blocks = merged.reshape(slots, size, width)
    rows = jnp.stack([pick(blocks, p, 0) for p in row_slot])
    corner = jnp.concatenate([corner[..., :width], corner[..., width:]], 1)

    def narrow(rows, corner, bit):
        second = bit_of(row, bit)
        other, extra = send_both(part(rows, 1, ~second), corner, "row", n_row, bit)
        rows = choose(part(rows, 1, second), other, row, row_owner, bit)
        return rows, choose(corner, extra, row, corner_rows, bit)

    def widen(x, axis, length, me, bit):
        return join(x, swap(x, axis, length, bit), 1, bit_of(me, bit))

    data = widen(data, "col", n_col, col, 2)
    data, corner = lax.optimization_barrier((data, corner))
    rows, corner = narrow(rows, corner, 2)
    data = widen(data, "col", n_col, col, 1)
    rows, corner = narrow(rows, corner, 4)
    corner = jnp.concatenate([corner[:, :thin], corner[:, thin:]], 2)
    data = jnp.concatenate([data, corner], 1)
    panels = lax.all_gather(data, "gz", axis=0)
    rows = choose(rows, swap(rows, "row", n_row, 1), row, row_owner, 1)
    for bit in (4, 2):
        rows = widen(rows, "row", n_row, row, bit)

    up0, term0 = first_terms(n_y, block_pattern, col_map, lower_inv, upper_inv, rows)
    return last_terms(n_y, slots, block_pattern, row_map, col_map, lower_inv, upper_inv, rows,
                      up0, term0, panels, merged)


def solution(mesh):
    in_specs = (P("gz", "row", "col"), P(), P(), P(), P(), P())
    out_specs = P("row", ("col", "gz"))
    return jax.shard_map(shards, mesh=mesh, in_specs=in_specs, out_specs=out_specs, check_vma=False)
```

```python
import functools

import jax
import jax.numpy as jnp
from jax import lax
from jax.experimental import pallas as pl
from jax.experimental.pallas import tpu as pltpu
from jax.sharding import PartitionSpec as P

VMEM = pl.BlockSpec(memory_space=pltpu.VMEM)
SMEM = pl.BlockSpec(memory_space=pltpu.SMEM)
PARAMS = pltpu.CompilerParams(vmem_limit_bytes=32 << 20)
LARGE = pltpu.CompilerParams(vmem_limit_bytes=60 << 20)


def position_of(table, value):
    iota = jnp.arange(table.shape[0], dtype=jnp.uint32)
    return jnp.sum(jnp.where(table == value, iota, 0), dtype=jnp.uint32)


def halves(a):
    high = a.astype(jnp.bfloat16)
    return high, (a - high.astype(jnp.float32)).astype(jnp.bfloat16)


def mm_halves(a, b):
    dot = functools.partial(jnp.dot, preferred_element_type=jnp.float32)
    return dot(a[0], b[0]) + (dot(a[0], b[1]) + dot(a[1], b[0]))


def mm(a, b):
    return mm_halves(halves(a), halves(b))


def find(ref, value):
    place = jnp.int32(0)
    for i in range(ref.shape[0]):
        place = jnp.where(ref[i] == value, i, place)
    return place


def panel_kernel(col_map, local, keep, give, buffer, sems):
    n_y, _, slots, thin, size = keep.shape
    core = lax.axis_index("gz") & 1
    copies = []
    for k in range(2):
        first = pl.multiple_of((find(col_map, k) & (slots - 1)) * size, size)
        copies.append(
            pltpu.make_async_copy(local.at[:, pl.ds(first, size)], buffer.at[k], sems.at[k])
        )
        copies[k].start()
    for k in range(2):
        copies[k].wait()
        for p in range(slots):
            for y in range(n_y):
                for out, which in ((keep, core), (give, 1 - core)):
                    first = pl.multiple_of(p * size + y * 2 * thin + which * thin, thin)
                    out[y, k, p] = buffer[k, pl.ds(first, thin), :].astype(jnp.float32)


def cut_panels(col_map, local, slots, n_y, thin, size):
    shape = jax.ShapeDtypeStruct((n_y, 2, slots, thin, size), jnp.float32)
    return pl.pallas_call(
        panel_kernel,
        out_shape=[shape, shape],
        in_specs=[SMEM, pl.BlockSpec(memory_space=pltpu.HBM)],
        out_specs=[VMEM, VMEM],
        scratch_shapes=[
            pltpu.VMEM((2, local.shape[0], size), jnp.bfloat16),
            pltpu.SemaphoreType.DMA((2,)),
        ],
        compiler_params=PARAMS,
    )(col_map, local)


def mask_at(block_pattern, row, col):
    return jnp.where(row == col, 1, block_pattern[row, col]).astype(jnp.float32)


def column_of(col_map, n_y):
    return col_map[lax.axis_index("col") * n_y + (lax.axis_index("gz") >> 1)]


def first_kernel(n_y, block_pattern, col_map, lower_inv, upper_inv, rows, up_out, term_out):
    col = column_of(col_map, n_y)
    mask = jnp.where(col > 0, mask_at(block_pattern, 0, col), 0.0)
    up = mask * mm(lower_inv[0], rows[0])
    up_out[...] = up
    term_out[...] = mm(upper_inv[0], up)


def first_terms(n_y, block_pattern, col_map, lower_inv, upper_inv, rows):
    shape = jax.ShapeDtypeStruct(rows.shape[1:], jnp.float32)
    return pl.pallas_call(
        functools.partial(first_kernel, n_y),
        out_shape=[shape, shape],
        in_specs=[SMEM] * 2 + [VMEM] * 3,
        out_specs=[VMEM, VMEM],
        compiler_params=PARAMS,
    )(block_pattern, col_map, lower_inv, upper_inv, rows)


def last_kernel(n_y, block_pattern, row_map, col_map, lower_inv, upper_inv, rows, up0, term0,
                merged, panels, out, high, low, buffer, sems):
    slots = high.shape[1] - 1
    size, width = up0.shape
    thin = size // (2 * n_y)
    core = lax.axis_index("gz") & 1
    col = column_of(col_map, n_y)
    copies = [
        pltpu.make_async_copy(panels.at[:, :, here, :], buffer.at[:, :, here, :], sems.at[i])
        for i, here in enumerate((pl.ds(slots * thin, thin), pl.ds(0, slots * thin)))
    ]
    for copy in copies:
        copy.start()

    def settle(p):
        for owner in range(2 * n_y):
            here = slice(owner * thin, (owner + 1) * thin)
            for k in range(2):
                a, b = halves(buffer[owner, k, p * thin : (p + 1) * thin, :])
                high[k, p, here, :] = a
                low[k, p, here, :] = b

    copies[0].wait()
    settle(slots)

    def stored(k, p):
        return high[k, p], low[k, p]

    lower0, lower1 = halves(lower_inv[0]), halves(lower_inv[1])
    upper0, upper1 = halves(upper_inv[0]), halves(upper_inv[1])
    up0 = up0[...]
    low_at = mask_at(block_pattern, 1, 0) * mm_halves(stored(0, slots), upper0)
    up_at = mask_at(block_pattern, 0, 1) * mm_halves(lower0, stored(1, slots))
    mask = jnp.where(col > 1, mask_at(block_pattern, 1, col), 0.0)
    up1 = mask * mm_halves(lower1, halves(rows[1] - mm(low_at, up0)))
    term1 = mm_halves(upper1, halves(up1))

    def own_half(matrix):
        left, right = matrix[:, :width], matrix[:, width:]
        return jnp.where(core == 0, left, right)

    term0 = jnp.where(col == 0, -own_half(upper_inv[0]), term0[...])
    term1 = jnp.where(col == 1, -own_half(upper_inv[1]), term1)
    term2 = mm_halves(upper0, halves(mm(up_at, term1)))
    both = halves(jnp.concatenate([term0, term2], axis=1))
    term1 = halves(term1)
    copies[1].wait()
    for p in range(slots):
        settle(p)
        row = row_map[lax.axis_index("row") * slots + p]
        own = mask_at(block_pattern, row, col)
        keep0 = jnp.where(row > 0, mask_at(block_pattern, row, 0), 0.0)
        keep1 = jnp.where(row > 1, mask_at(block_pattern, row, 1), 0.0)
        panel0 = (col == 0) & (row > 0)
        panel1 = (col == 1) & (row > 1)
        scale = jnp.where(panel0 | panel1, 0.0, own)
        scale0 = jnp.where(panel0, keep0, scale * keep0)
        scale1 = jnp.where(panel1, keep1, scale * keep1)
        two = mm_halves(stored(0, p), both)
        one = mm_halves(stored(1, p), term1)
        here = slice(p * size, (p + 1) * size)
        value = (
            scale * merged[here, :]
            - scale0 * two[:, :width]
            - scale1 * (one - keep0 * two[:, width:])
        )
        value = jnp.where((row == 0) & (col > 0), up0, value)
        value = jnp.where((row == 1) & (col > 1), up1, value)
        out[here, :] = value.astype(jnp.bfloat16)


def last_terms(n_y, slots, block_pattern, row_map, col_map, lower_inv, upper_inv, rows, up0, term0,
               panels, merged):
    size = lower_inv.shape[-1]
    return pl.pallas_call(
        functools.partial(last_kernel, n_y),
        out_shape=jax.ShapeDtypeStruct(merged.shape, jnp.bfloat16),
        in_specs=[SMEM] * 3 + [VMEM] * 6 + [pl.BlockSpec(memory_space=pltpu.HBM)],
        out_specs=VMEM,
        scratch_shapes=[
            pltpu.VMEM((2, slots + 1, size, size), jnp.bfloat16),
            pltpu.VMEM((2, slots + 1, size, size), jnp.bfloat16),
            pltpu.VMEM(panels.shape, jnp.float32),
            pltpu.SemaphoreType.DMA((2,)),
        ],
        compiler_params=LARGE,
    )(block_pattern, row_map, col_map, lower_inv, upper_inv, rows, up0, term0, merged, panels)


def swap(x, axis, size, bit):
    return lax.ppermute(x, axis, [(i, i ^ bit) for i in range(size)])


def bit_of(index, bit):
    return (index & jnp.uint32(bit)) != 0


def select(index, values):
    out = values[0]
    for i in range(1, len(values)):
        out = jnp.where(index == i, values[i], out)
    return out


def choose(mine, other, me, sources, bit):
    same = [bit_of(me, bit) == bit_of(s, bit) for s in sources]
    return jnp.stack([jnp.where(same[k], mine[k], other[k]) for k in range(2)])


def choose_of_four(values, me, sources):
    return jnp.stack([select(me ^ s, [v[k] for v in values]) for k, s in enumerate(sources)])


def pick(x, index, axis):
    return lax.dynamic_index_in_dim(x, index, axis, keepdims=False)


def shards(contributions, block_pattern, row_map, col_map, lower_inv, upper_inv):
    size = upper_inv.shape[-1]
    local = contributions[0]
    slots = local.shape[0] // size
    n_gz, n_row, n_col = lax.axis_size("gz"), lax.axis_size("row"), lax.axis_size("col")
    gz, row, col = [lax.axis_index(a).astype(jnp.uint32) for a in ("gz", "row", "col")]
    y, core = gz >> 1, gz & 1
    n_y = n_gz // 2
    thin = size // n_gz
    width = local.shape[1] // n_gz
    row_at = [position_of(row_map, k) for k in range(2)]
    col_at = [position_of(col_map, k) for k in range(2)]
    shift = slots.bit_length() - 1
    row_owner = [p >> shift for p in row_at]
    col_owner = [p >> shift for p in col_at]
    row_slot = [p & (slots - 1) for p in row_at]
    def around(step):
        return [(2 * i + c, 2 * ((i + step) % n_y) + c) for i in range(n_y) for c in range(2)]

    keep, give = cut_panels(col_map, local, slots, n_y, thin, size)
    other = swap(give, "gz", n_gz, 1)
    other, local = lax.optimization_barrier((other, local))
    parts = keep + other
    arrived = [
        lax.ppermute(pick(parts, (y + step) & (n_y - 1), 0), "gz", around(step))
        for step in (1, 3, 2)
    ]
    panel = pick(parts, y, 0) + (arrived[0] + arrived[1] + arrived[2])

    merged = lax.psum_scatter(local.astype(jnp.float32), "gz", scatter_dimension=1, tiled=True)

    corner = jnp.stack([pick(panel[k], row_slot[1 - k], 0) for k in range(2)])
    data = panel.reshape(2, slots * thin, size)

    def split_four(data, extra, me, sources, axis, length, unit, extra_sources=None):
        quarter = data.shape[1] // 4
        kept, extras = [], []
        for d in range(4):
            chunk = lax.dynamic_slice_in_dim(data, (me ^ d) * quarter, quarter, 1)
            both = jnp.concatenate([chunk, extra], 1)
            if d:
                both = swap(both, axis, length, d * unit)
            kept.append(both[:, :quarter])
            extras.append(both[:, quarter:])
        return choose_of_four(kept, me, sources), choose_of_four(extras, me, extra_sources or sources)

    def join_four(data, me, axis, length, unit):
        parts = [data] + [swap(data, axis, length, d * unit) for d in range(1, 4)]
        return jnp.concatenate([select(me ^ i, parts) for i in range(4)], 1)

    col_member, row_member = col & 3, row >> 1
    col_sources = [c & 3 for c in col_owner]
    data, corner = split_four(data, corner, col_member, col_sources, "col", n_col, 1)
    thick = data.shape[1]
    both = jnp.concatenate([data, corner], 1)
    both = choose(both, swap(both, "col", n_col, 4), col, col_owner, 4)
    data, corner = both[:, :thick], both[:, thick:]

    corner_rows = row_owner[::-1]
    mirror = [
        (r * n_col + c, (r ^ 1) * n_col + c ^ (n_col - 1))
        for r in range(n_row)
        for c in range(n_col)
    ]
    corner = choose(corner, lax.ppermute(corner, ("row", "col"), mirror), row, corner_rows, 1)

    blocks = merged.reshape(slots, size, width)
    rows = jnp.stack([pick(blocks, p, 0) for p in row_slot])
    corner = jnp.concatenate([corner[..., :width], corner[..., width:]], 1)

    data = join_four(data, col_member, "col", n_col, 1)
    rows, corner = split_four(
        rows, corner, row_member, [r >> 1 for r in row_owner], "row", n_row, 2,
        [r >> 1 for r in corner_rows],
    )
    corner = jnp.concatenate([corner[:, :thin], corner[:, thin:]], 2)
    data = jnp.concatenate([data, corner], 1)
    panels = lax.all_gather(data, "gz", axis=0)
    rows = choose(rows, swap(rows, "row", n_row, 1), row, row_owner, 1)
    rows = join_four(rows, row_member, "row", n_row, 2)

    up0, term0 = first_terms(n_y, block_pattern, col_map, lower_inv, upper_inv, rows)
    return last_terms(n_y, slots, block_pattern, row_map, col_map, lower_inv, upper_inv, rows,
                      up0, term0, panels, merged)


def solution(mesh):
    in_specs = (P("gz", "row", "col"), P(), P(), P(), P(), P())
    out_specs = P("row", ("col", "gz"))
    return jax.shard_map(shards, mesh=mesh, in_specs=in_specs, out_specs=out_specs, check_vma=False)
```

```python
import functools

import jax
import jax.numpy as jnp
from jax import lax
from jax.experimental import pallas as pl
from jax.experimental.pallas import tpu as pltpu
from jax.sharding import PartitionSpec as P

VMEM = pl.BlockSpec(memory_space=pltpu.VMEM)
SMEM = pl.BlockSpec(memory_space=pltpu.SMEM)
PARAMS = pltpu.CompilerParams(vmem_limit_bytes=32 << 20)
LARGE = pltpu.CompilerParams(vmem_limit_bytes=50 << 20)


def position_of(table, value):
    iota = jnp.arange(table.shape[0], dtype=jnp.uint32)
    return jnp.sum(jnp.where(table == value, iota, 0), dtype=jnp.uint32)


def halves(a):
    high = a.astype(jnp.bfloat16)
    return high, (a - high.astype(jnp.float32)).astype(jnp.bfloat16)


def mm_halves(a, b):
    dot = functools.partial(jnp.dot, preferred_element_type=jnp.float32)
    return dot(a[0], b[0]) + (dot(a[0], b[1]) + dot(a[1], b[0]))


def mm(a, b):
    return mm_halves(halves(a), halves(b))


def find(ref, value):
    place = jnp.int32(0)
    for i in range(ref.shape[0]):
        place = jnp.where(ref[i] == value, i, place)
    return place


def panel_kernel(col_map, local, keep, give, buffer, sems):
    n_y, _, slots, thin, size = keep.shape
    core = lax.axis_index("gz") & 1
    copies = []
    for k in range(2):
        first = pl.multiple_of((find(col_map, k) & (slots - 1)) * size, size)
        copies.append(
            pltpu.make_async_copy(local.at[:, pl.ds(first, size)], buffer.at[k], sems.at[k])
        )
        copies[k].start()
    for k in range(2):
        copies[k].wait()
        for p in range(slots):
            for y in range(n_y):
                for out, which in ((keep, core), (give, 1 - core)):
                    first = pl.multiple_of(p * size + y * 2 * thin + which * thin, thin)
                    out[y, k, p] = buffer[k, pl.ds(first, thin), :].astype(jnp.float32)


def cut_panels(col_map, local, slots, n_y, thin, size):
    shape = jax.ShapeDtypeStruct((n_y, 2, slots, thin, size), jnp.float32)
    return pl.pallas_call(
        panel_kernel,
        out_shape=[shape, shape],
        in_specs=[SMEM, pl.BlockSpec(memory_space=pltpu.HBM)],
        out_specs=[VMEM, VMEM],
        scratch_shapes=[
            pltpu.VMEM((2, local.shape[0], size), jnp.bfloat16),
            pltpu.SemaphoreType.DMA((2,)),
        ],
        compiler_params=PARAMS,
    )(col_map, local)


def mask_at(block_pattern, row, col):
    return jnp.where(row == col, 1, block_pattern[row, col]).astype(jnp.float32)


def column_of(col_map, n_y):
    return col_map[lax.axis_index("col") * n_y + (lax.axis_index("gz") >> 1)]


def product_kernel(upper_inv, lower_inv, out):
    for k in range(2):
        out[k] = mm(upper_inv[k], lower_inv[k])


def products(upper_inv, lower_inv):
    return pl.pallas_call(
        product_kernel,
        out_shape=jax.ShapeDtypeStruct(lower_inv.shape, jnp.float32),
        in_specs=[VMEM, VMEM],
        out_specs=VMEM,
        compiler_params=PARAMS,
    )(upper_inv, lower_inv)


def first_kernel(n_y, block_pattern, col_map, lower_inv, upper_inv, rows, up_out, term_out):
    col = column_of(col_map, n_y)
    mask = jnp.where(col > 0, mask_at(block_pattern, 0, col), 0.0)
    up = mask * mm(lower_inv[0], rows[0])
    up_out[...] = up
    term_out[...] = mm(upper_inv[0], up)


def first_terms(n_y, block_pattern, col_map, lower_inv, upper_inv, rows):
    shape = jax.ShapeDtypeStruct(rows.shape[1:], jnp.float32)
    return pl.pallas_call(
        functools.partial(first_kernel, n_y),
        out_shape=[shape, shape],
        in_specs=[SMEM] * 2 + [VMEM] * 3,
        out_specs=[VMEM, VMEM],
        compiler_params=PARAMS,
    )(block_pattern, col_map, lower_inv, upper_inv, rows)


def last_kernel(n_y, block_pattern, row_map, col_map, lower_inv, upper_inv, both_inv, rows, up0,
                term0, merged, panels, out, high, low, buffer, sems):
    slots = high.shape[1] - 1
    size, width = up0.shape
    thin = size // (2 * n_y)
    core = lax.axis_index("gz") & 1
    col = column_of(col_map, n_y)
    copies = [
        pltpu.make_async_copy(panels.at[:, :, here, :], buffer.at[:, :, here, :], sems.at[i])
        for i, here in enumerate((pl.ds(slots * thin, thin), pl.ds(0, slots * thin)))
    ]
    for copy in copies:
        copy.start()

    def settle(p):
        for owner in range(2 * n_y):
            here = slice(owner * thin, (owner + 1) * thin)
            for k in range(2):
                a, b = halves(buffer[owner, k, p * thin : (p + 1) * thin, :])
                high[k, p, here, :] = a
                low[k, p, here, :] = b

    copies[0].wait()
    settle(slots)

    def stored(k, p):
        return high[k, p], low[k, p]

    up0, term0 = up0[...], term0[...]
    mask = jnp.where(col > 1, mask_at(block_pattern, 1, col), 0.0)
    reduced = halves(rows[1] - mask_at(block_pattern, 1, 0) * mm_halves(stored(0, slots), halves(term0)))
    term1 = mask * mm_halves(halves(both_inv[1]), reduced)
    up1 = mask * mm_halves(halves(lower_inv[1]), reduced)

    def own_half(matrix):
        left, right = matrix[:, :width], matrix[:, width:]
        return jnp.where(core == 0, left, right)

    term0 = jnp.where(col == 0, -own_half(upper_inv[0]), term0)
    term1 = jnp.where(col == 1, -own_half(upper_inv[1]), term1)
    term1 = halves(term1)
    term2 = mask_at(block_pattern, 0, 1) * mm(both_inv[0], mm_halves(stored(1, slots), term1))
    both = halves(jnp.concatenate([term0, term2], axis=1))
    copies[1].wait()
    for p in range(slots):
        settle(p)
        row = row_map[lax.axis_index("row") * slots + p]
        own = mask_at(block_pattern, row, col)
        keep0 = jnp.where(row > 0, mask_at(block_pattern, row, 0), 0.0)
        keep1 = jnp.where(row > 1, mask_at(block_pattern, row, 1), 0.0)
        panel0 = (col == 0) & (row > 0)
        panel1 = (col == 1) & (row > 1)
        scale = jnp.where(panel0 | panel1, 0.0, own)
        scale0 = jnp.where(panel0, keep0, scale * keep0)
        scale1 = jnp.where(panel1, keep1, scale * keep1)
        two = mm_halves(stored(0, p), both)
        one = mm_halves(stored(1, p), term1)
        here = slice(p * size, (p + 1) * size)
        value = (
            scale * merged[here, :]
            - scale0 * two[:, :width]
            - scale1 * (one - keep0 * two[:, width:])
        )
        value = jnp.where((row == 0) & (col > 0), up0, value)
        value = jnp.where((row == 1) & (col > 1), up1, value)
        out[here, :] = value.astype(jnp.bfloat16)


def last_terms(n_y, slots, block_pattern, row_map, col_map, lower_inv, upper_inv, both_inv, rows,
               up0, term0, panels, merged):
    size = lower_inv.shape[-1]
    return pl.pallas_call(
        functools.partial(last_kernel, n_y),
        out_shape=jax.ShapeDtypeStruct(merged.shape, jnp.bfloat16),
        in_specs=[SMEM] * 3 + [VMEM] * 7 + [pl.BlockSpec(memory_space=pltpu.HBM)],
        out_specs=VMEM,
        scratch_shapes=[
            pltpu.VMEM((2, slots + 1, size, size), jnp.bfloat16),
            pltpu.VMEM((2, slots + 1, size, size), jnp.bfloat16),
            pltpu.VMEM(panels.shape, jnp.float32),
            pltpu.SemaphoreType.DMA((2,)),
        ],
        compiler_params=LARGE,
    )(block_pattern, row_map, col_map, lower_inv, upper_inv, both_inv, rows, up0, term0, merged,
      panels)


def swap(x, axis, size, bit):
    return lax.ppermute(x, axis, [(i, i ^ bit) for i in range(size)])


def bit_of(index, bit):
    return (index & jnp.uint32(bit)) != 0


def part(x, axis, second):
    half = x.shape[axis] // 2
    return lax.dynamic_slice_in_dim(x, second.astype(jnp.uint32) * half, half, axis)


def join(mine, other, axis, second):
    return jnp.where(
        second,
        jnp.concatenate([other, mine], axis),
        jnp.concatenate([mine, other], axis),
    )


def choose(mine, other, me, sources, bit):
    same = [bit_of(me, bit) == bit_of(s, bit) for s in sources]
    return jnp.stack([jnp.where(same[k], mine[k], other[k]) for k in range(len(sources))])


def pick(x, index, axis):
    return lax.dynamic_index_in_dim(x, index, axis, keepdims=False)


def shards(contributions, block_pattern, row_map, col_map, lower_inv, upper_inv):
    size = upper_inv.shape[-1]
    local = contributions[0]
    slots = local.shape[0] // size
    n_gz, n_row, n_col = lax.axis_size("gz"), lax.axis_size("row"), lax.axis_size("col")
    gz, row, col = [lax.axis_index(a).astype(jnp.uint32) for a in ("gz", "row", "col")]
    y, core = gz >> 1, gz & 1
    n_y = n_gz // 2
    thin = size // n_gz
    width = local.shape[1] // n_gz
    row_at = [position_of(row_map, k) for k in range(2)]
    col_at = [position_of(col_map, k) for k in range(2)]
    shift = slots.bit_length() - 1
    row_owner = [p >> shift for p in row_at]
    col_owner = [p >> shift for p in col_at]
    row_slot = [p & (slots - 1) for p in row_at]
    def around(step):
        return [(2 * i + c, 2 * ((i + step) % n_y) + c) for i in range(n_y) for c in range(2)]

    keep, give = cut_panels(col_map, local, slots, n_y, thin, size)
    other = swap(give, "gz", n_gz, 1)
    other, local = lax.optimization_barrier((other, local))
    parts = keep + other
    arrived = [
        lax.ppermute(pick(parts, (y + step) & (n_y - 1), 0), "gz", around(step))
        for step in (1, 3, 2)
    ]
    both_inv, arrived = lax.optimization_barrier((products(upper_inv, lower_inv), arrived))
    panel = pick(parts, y, 0) + (arrived[0] + arrived[1] + arrived[2])

    merged = lax.psum_scatter(local.astype(jnp.float32), "gz", scatter_dimension=1, tiled=True)

    corner_rows = row_owner[::-1]
    corner = jnp.stack([pick(panel[k], row_slot[1 - k], 0) for k in range(2)])
    for bit in (2, 4):
        corner = choose(corner, swap(corner, "row", n_row, bit), row, corner_rows, bit)
    mirror = [
        (r * n_col + c, (r ^ 1) * n_col + c ^ (n_col - 1))
        for r in range(n_row)
        for c in range(n_col)
    ]
    corner_other = lax.ppermute(corner, ("row", "col"), mirror)
    corner = choose(corner, corner_other, row, corner_rows, 1)
    corner_owner = [
        jnp.where(bit_of(row, 1) == bit_of(corner_rows[k], 1), c, c ^ (n_col - 1))
        for k, c in enumerate(col_owner)
    ]

    data = panel.reshape(2, slots * thin, size)
    for bit in (1, 2, 4):
        mine = data
        if bit < 4:
            second = bit_of(col, bit)
            mine, data = part(data, 1, second), part(data, 1, ~second)
        data = choose(mine, swap(data, "col", n_col, bit), col, col_owner, bit)
    corner = choose(corner, swap(corner, "col", n_col, 4), col, corner_owner, 4)

    blocks = merged.reshape(slots, size, width)
    rows = jnp.stack([pick(blocks, p, 0) for p in row_slot])

    def narrow(rows, bit):
        second = bit_of(row, bit)
        other = swap(part(rows, 1, ~second), "row", n_row, bit)
        return choose(part(rows, 1, second), other, row, row_owner, bit)

    def widen(x, other, me, bit):
        return join(x, other, 1, bit_of(me, bit))

    def send_both(data, corner, bit):
        other = swap(jnp.concatenate([data, corner], 1), "col", n_col, bit)
        thick = data.shape[1]
        return other[:, :thick], choose(corner, other[:, thick:], col, corner_owner, bit)

    rows = narrow(rows, 2)
    other, corner = send_both(data, corner, 2)
    data = widen(data, other, col, 2)
    data, rows = lax.optimization_barrier((data, rows))
    rows = narrow(rows, 4)
    other, corner = send_both(data, corner, 1)
    data = jnp.concatenate([widen(data, other, col, 1), corner], 1)
    data, rows = lax.optimization_barrier((data, rows))
    panels = lax.all_gather(data, "gz", axis=0)
    rows = choose(rows, swap(rows, "row", n_row, 1), row, row_owner, 1)
    for bit in (4, 2):
        rows = widen(rows, swap(rows, "row", n_row, bit), row, bit)

    up0, term0 = first_terms(n_y, block_pattern, col_map, lower_inv, upper_inv, rows)
    return last_terms(n_y, slots, block_pattern, row_map, col_map, lower_inv, upper_inv, both_inv,
                      rows, up0, term0, panels, merged)


def solution(mesh):
    in_specs = (P("gz", "row", "col"), P(), P(), P(), P(), P())
    out_specs = P("row", ("col", "gz"))
    return jax.shard_map(shards, mesh=mesh, in_specs=in_specs, out_specs=out_specs, check_vma=False)
```

```python
import functools

import jax
import jax.numpy as jnp
from jax import lax
from jax.experimental import pallas as pl
from jax.experimental.pallas import tpu as pltpu
from jax.sharding import PartitionSpec as P

VMEM = pl.BlockSpec(memory_space=pltpu.VMEM)
SMEM = pl.BlockSpec(memory_space=pltpu.SMEM)
PARAMS = pltpu.CompilerParams(vmem_limit_bytes=32 << 20)
MIDDLE = pltpu.CompilerParams(vmem_limit_bytes=50 << 20)
LARGE = pltpu.CompilerParams(vmem_limit_bytes=60 << 20)


def position_of(table, value):
    iota = jnp.arange(table.shape[0], dtype=jnp.uint32)
    return jnp.sum(jnp.where(table == value, iota, 0), dtype=jnp.uint32)


def halves(a):
    high = a.astype(jnp.bfloat16)
    return high, (a - high.astype(jnp.float32)).astype(jnp.bfloat16)


def mm_halves(a, b):
    dot = functools.partial(jnp.dot, preferred_element_type=jnp.float32)
    return dot(a[0], b[0]) + (dot(a[0], b[1]) + dot(a[1], b[0]))


def mm(a, b):
    return mm_halves(halves(a), halves(b))


def find(ref, value):
    place = jnp.int32(0)
    for i in range(ref.shape[0]):
        place = jnp.where(ref[i] == value, i, place)
    return place


def panel_kernel(col_map, local, keep, give, buffer, sems):
    n_y, _, slots, thin, size = keep.shape
    core = lax.axis_index("gz") & 1
    copies = []
    for k in range(2):
        first = pl.multiple_of((find(col_map, k) & (slots - 1)) * size, size)
        copies.append(
            pltpu.make_async_copy(local.at[:, pl.ds(first, size)], buffer.at[k], sems.at[k])
        )
        copies[k].start()
    for k in range(2):
        copies[k].wait()
        for p in range(slots):
            for y in range(n_y):
                for out, which in ((keep, core), (give, 1 - core)):
                    first = pl.multiple_of(p * size + y * 2 * thin + which * thin, thin)
                    out[y, k, p] = buffer[k, pl.ds(first, thin), :].astype(jnp.float32)


def cut_panels(col_map, local, slots, n_y, thin, size):
    shape = jax.ShapeDtypeStruct((n_y, 2, slots, thin, size), jnp.float32)
    return pl.pallas_call(
        panel_kernel,
        out_shape=[shape, shape],
        in_specs=[SMEM, pl.BlockSpec(memory_space=pltpu.HBM)],
        out_specs=[VMEM, VMEM],
        scratch_shapes=[
            pltpu.VMEM((2, local.shape[0], size), jnp.bfloat16),
            pltpu.SemaphoreType.DMA((2,)),
        ],
        compiler_params=LARGE,
    )(col_map, local)


def mask_at(block_pattern, row, col):
    return jnp.where(row == col, 1, block_pattern[row, col]).astype(jnp.float32)


def column_of(col_map, n_y):
    return col_map[lax.axis_index("col") * n_y + (lax.axis_index("gz") >> 1)]


def first_kernel(n_y, block_pattern, col_map, lower_inv, upper_inv, rows, up_out, term_out):
    col = column_of(col_map, n_y)
    mask = jnp.where(col > 0, mask_at(block_pattern, 0, col), 0.0)
    up = mask * mm(lower_inv[0], rows[0])
    up_out[...] = up
    term_out[...] = mm(upper_inv[0], up)


def first_terms(n_y, block_pattern, col_map, lower_inv, upper_inv, rows):
    shape = jax.ShapeDtypeStruct(rows.shape[1:], jnp.float32)
    return pl.pallas_call(
        functools.partial(first_kernel, n_y),
        out_shape=[shape, shape],
        in_specs=[SMEM] * 2 + [VMEM] * 3,
        out_specs=[VMEM, VMEM],
        compiler_params=PARAMS,
    )(block_pattern, col_map, lower_inv, upper_inv, rows)


def last_kernel(n_y, block_pattern, row_map, col_map, lower_inv, upper_inv, rows, up0, term0,
                merged, panels, out, high, low, buffer, sems):
    slots = high.shape[1] - 1
    size, width = up0.shape
    thin = size // (2 * n_y)
    core = lax.axis_index("gz") & 1
    col = column_of(col_map, n_y)
    copies = [
        pltpu.make_async_copy(panels.at[:, :, here, :], buffer.at[:, :, here, :], sems.at[i])
        for i, here in enumerate((pl.ds(slots * thin, thin), pl.ds(0, slots * thin)))
    ]
    for copy in copies:
        copy.start()

    def settle(p):
        for owner in range(2 * n_y):
            here = slice(owner * thin, (owner + 1) * thin)
            for k in range(2):
                a, b = halves(buffer[owner, k, p * thin : (p + 1) * thin, :])
                high[k, p, here, :] = a
                low[k, p, here, :] = b

    copies[0].wait()
    settle(slots)

    def stored(k, p):
        return high[k, p], low[k, p]

    lower0, lower1 = halves(lower_inv[0]), halves(lower_inv[1])
    upper0, upper1 = halves(upper_inv[0]), halves(upper_inv[1])
    up0 = up0[...]
    low_at = mask_at(block_pattern, 1, 0) * mm_halves(stored(0, slots), upper0)
    up_at = mask_at(block_pattern, 0, 1) * mm_halves(lower0, stored(1, slots))
    mask = jnp.where(col > 1, mask_at(block_pattern, 1, col), 0.0)
    up1 = mask * mm_halves(lower1, halves(rows[1] - mm(low_at, up0)))
    term1 = mm_halves(upper1, halves(up1))

    def own_half(matrix):
        left, right = matrix[:, :width], matrix[:, width:]
        return jnp.where(core == 0, left, right)

    term0 = jnp.where(col == 0, -own_half(upper_inv[0]), term0[...])
    term1 = jnp.where(col == 1, -own_half(upper_inv[1]), term1)
    term2 = mm_halves(upper0, halves(mm(up_at, term1)))
    both = halves(jnp.concatenate([term0, term2], axis=1))
    term1 = halves(term1)
    copies[1].wait()
    for p in range(slots):
        settle(p)
        row = row_map[lax.axis_index("row") * slots + p]
        own = mask_at(block_pattern, row, col)
        keep0 = jnp.where(row > 0, mask_at(block_pattern, row, 0), 0.0)
        keep1 = jnp.where(row > 1, mask_at(block_pattern, row, 1), 0.0)
        panel0 = (col == 0) & (row > 0)
        panel1 = (col == 1) & (row > 1)
        scale = jnp.where(panel0 | panel1, 0.0, own)
        scale0 = jnp.where(panel0, keep0, scale * keep0)
        scale1 = jnp.where(panel1, keep1, scale * keep1)
        two = mm_halves(stored(0, p), both)
        one = mm_halves(stored(1, p), term1)
        here = slice(p * size, (p + 1) * size)
        value = (
            scale * merged[here, :]
            - scale0 * two[:, :width]
            - scale1 * (one - keep0 * two[:, width:])
        )
        value = jnp.where((row == 0) & (col > 0), up0, value)
        value = jnp.where((row == 1) & (col > 1), up1, value)
        out[here, :] = value.astype(jnp.bfloat16)


def last_terms(n_y, slots, block_pattern, row_map, col_map, lower_inv, upper_inv, rows, up0, term0,
               panels, merged):
    size = lower_inv.shape[-1]
    return pl.pallas_call(
        functools.partial(last_kernel, n_y),
        out_shape=jax.ShapeDtypeStruct(merged.shape, jnp.bfloat16),
        in_specs=[SMEM] * 3 + [VMEM] * 6 + [pl.BlockSpec(memory_space=pltpu.HBM)],
        out_specs=VMEM,
        scratch_shapes=[
            pltpu.VMEM((2, slots + 1, size, size), jnp.bfloat16),
            pltpu.VMEM((2, slots + 1, size, size), jnp.bfloat16),
            pltpu.VMEM(panels.shape, jnp.float32),
            pltpu.SemaphoreType.DMA((2,)),
        ],
        compiler_params=MIDDLE,
    )(block_pattern, row_map, col_map, lower_inv, upper_inv, rows, up0, term0, merged, panels)


def swap(x, axis, size, bit):
    return lax.ppermute(x, axis, [(i, i ^ bit) for i in range(size)])


def bit_of(index, bit):
    return (index & jnp.uint32(bit)) != 0


def part(x, axis, second):
    half = x.shape[axis] // 2
    return lax.dynamic_slice_in_dim(x, second.astype(jnp.uint32) * half, half, axis)


def join(mine, other, axis, second):
    return jnp.where(
        second,
        jnp.concatenate([other, mine], axis),
        jnp.concatenate([mine, other], axis),
    )


def choose(mine, other, me, sources, bit):
    same = [bit_of(me, bit) == bit_of(s, bit) for s in sources]
    return jnp.stack([jnp.where(same[k], mine[k], other[k]) for k in range(len(sources))])


def pick(x, index, axis):
    return lax.dynamic_index_in_dim(x, index, axis, keepdims=False)


def shards(contributions, block_pattern, row_map, col_map, lower_inv, upper_inv):
    size = upper_inv.shape[-1]
    local = contributions[0]
    slots = local.shape[0] // size
    n_gz, n_row, n_col = lax.axis_size("gz"), lax.axis_size("row"), lax.axis_size("col")
    gz, row, col = [lax.axis_index(a).astype(jnp.uint32) for a in ("gz", "row", "col")]
    y, core = gz >> 1, gz & 1
    n_y = n_gz // 2
    thin = size // n_gz
    width = local.shape[1] // n_gz
    row_at = [position_of(row_map, k) for k in range(2)]
    col_at = [position_of(col_map, k) for k in range(2)]
    shift = slots.bit_length() - 1
    row_owner = [p >> shift for p in row_at]
    col_owner = [p >> shift for p in col_at]
    row_slot = [p & (slots - 1) for p in row_at]
    def around(step):
        return [(2 * i + c, 2 * ((i + step) % n_y) + c) for i in range(n_y) for c in range(2)]

    keep, give = cut_panels(col_map, local, slots, n_y, thin, size)
    other = swap(give, "gz", n_gz, 1)
    other, local = lax.optimization_barrier((other, local))
    parts = keep + other
    panel = pick(parts, y, 0)
    for step in (1, 3, 2):
        chunk = pick(parts, (y + step) & (n_y - 1), 0)
        panel = panel + lax.ppermute(chunk, "gz", around(step))

    merged = lax.psum_scatter(local.astype(jnp.float32), "gz", scatter_dimension=1, tiled=True)

    corner_rows = row_owner[::-1]
    corner = jnp.stack([pick(panel[k], row_slot[1 - k], 0) for k in range(2)])
    for bit in (2, 4):
        corner = choose(corner, swap(corner, "row", n_row, bit), row, corner_rows, bit)
    mirror = [
        (r * n_col + c, (r ^ 1) * n_col + c ^ (n_col - 1))
        for r in range(n_row)
        for c in range(n_col)
    ]
    corner_other = lax.ppermute(corner, ("row", "col"), mirror)
    corner = choose(corner, corner_other, row, corner_rows, 1)
    corner_owner = [
        jnp.where(bit_of(row, 1) == bit_of(corner_rows[k], 1), c, c ^ (n_col - 1))
        for k, c in enumerate(col_owner)
    ]

    data = panel.reshape(2, slots * thin, size)
    for bit in (1, 2, 4):
        mine = data
        if bit < 4:
            second = bit_of(col, bit)
            mine, data = part(data, 1, second), part(data, 1, ~second)
        data = choose(mine, swap(data, "col", n_col, bit), col, col_owner, bit)
    corner = choose(corner, swap(corner, "col", n_col, 4), col, corner_owner, 4)

    blocks = merged.reshape(slots, size, width)
    rows = jnp.stack([pick(blocks, p, 0) for p in row_slot])

    def narrow(rows, bit):
        second = bit_of(row, bit)
        other = swap(part(rows, 1, ~second), "row", n_row, bit)
        return choose(part(rows, 1, second), other, row, row_owner, bit)

    def widen(x, other, me, bit):
        return join(x, other, 1, bit_of(me, bit))

    def send_both(data, corner, bit):
        other = swap(jnp.concatenate([data, corner], 1), "col", n_col, bit)
        thick = data.shape[1]
        return other[:, :thick], choose(corner, other[:, thick:], col, corner_owner, bit)

    rows = narrow(rows, 2)
    other, corner = send_both(data, corner, 2)
    data = widen(data, other, col, 2)
    data, rows = lax.optimization_barrier((data, rows))
    rows = narrow(rows, 4)
    other, corner = send_both(data, corner, 1)
    data = jnp.concatenate([widen(data, other, col, 1), corner], 1)
    data, rows = lax.optimization_barrier((data, rows))
    panels = lax.all_gather(data, "gz", axis=0)
    rows = choose(rows, swap(rows, "row", n_row, 1), row, row_owner, 1)
    for bit in (4, 2):
        rows = widen(rows, swap(rows, "row", n_row, bit), row, bit)

    up0, term0 = first_terms(n_y, block_pattern, col_map, lower_inv, upper_inv, rows)
    return last_terms(n_y, slots, block_pattern, row_map, col_map, lower_inv, upper_inv, rows,
                      up0, term0, panels, merged)


def solution(mesh):
    in_specs = (P("gz", "row", "col"), P(), P(), P(), P(), P())
    out_specs = P("row", ("col", "gz"))
    return jax.shard_map(shards, mesh=mesh, in_specs=in_specs, out_specs=out_specs, check_vma=False)
```
